32 devices in a mesh: shift: 4 (over x, core), space: 8 (over z, y).
Axes of the slice: x: 2, y: 2, z: 4, core: 2. Of those that a mesh axis runs over, the one named last changes fastest.
Arguments:
- labels: int32 [16, 32, 256], P('space'), may hold values from 0 to 7
- conductance: float32 [8], replicated, may hold values from 0.2 to 5
- capacity_table: float32 [8], replicated, may hold values from 0.5 to 2
- shift_values: float32 [8], replicated, may hold values from 0.1 to 4
- prior_basis: float32 [256, 16, 32, 256], P(None, 'space', 'shift'), may hold values from -6 to 6
Outputs:
- new_block: float32 [8, 8, 16, 32, 256], P(None, None, 'space', 'shift')
- coefficients: float32 [64, 256], replicated
- factor: float32 [64, 64], replicated
The draws below stay inside these ranges and needn't reach their ends.
All inputs are finite; a program needn't handle non-finite values.
Results may differ from the reference program's by a relative error of at most 0.0003.
Values sent between devices are 32-bit elements; how exact they have to be, the bound alone decides.
A program may use at most 64 MiB of HBM per device.

```python
import math
import jax
import jax.numpy as jnp
from jax import lax

NY = 32
NZ = 256
COLS = 8
BASIS = 256
SWEEPS = 4
MATS = 8
SHIFTS = 8
NEW = 64
NX = 16


def draw_basis_values(key):
    first_key, second_key, third_key = jax.random.split(jax.random.fold_in(key, 17), 3)
    scales = jnp.exp(jax.random.uniform(first_key, (BASIS, 1), jnp.float32, jnp.log(0.6), jnp.log(1.5)))
    values = jax.random.truncated_normal(second_key, -4.0, 4.0, (BASIS, NX * NY * NZ), jnp.float32)
    mixing = jnp.eye(BASIS, dtype=jnp.float32) + 0.5 * BASIS ** (-0.5) * jax.random.normal(third_key, (BASIS, BASIS), jnp.float32)
    mixed = jnp.dot(mixing, values, precision=lax.Precision.HIGHEST) * scales
    return jnp.clip(mixed, -6.0, 6.0).reshape(BASIS, NX, NY, NZ)


def draw_prior_basis(key, part):
    return draw_basis_values(key)


def plant(array, own_key, least, high):
    longest = array.shape.index(max(array.shape))
    spots = []
    for shift in (0, 1):
        where = [jax.random.randint(jax.random.fold_in(own_key, axis), (), 0, length) for axis, length in enumerate(array.shape)]
        where[longest] = (where[longest] + shift) % array.shape[longest]
        spots.append(tuple(where))
    return array.at[spots[0]].set(least).at[spots[1]].set(high)


def setup_inputs(seed: int = 0) -> dict:
    seeds = jax.random.split(jax.random.key(seed), 6)
    return {
        "labels": plant(jax.random.randint(seeds[0], (NX, NY, NZ), 0, MATS), jax.random.fold_in(seeds[0], 1), 0, MATS - 1).astype(jnp.int32),
        "conductance": jnp.clip(jnp.exp(jax.random.uniform(seeds[1], (MATS,), jnp.float32, math.log(0.2), math.log(5.0))), 0.2, 5.0),
        "capacity_table": jnp.clip(jnp.exp(jax.random.uniform(seeds[2], (MATS,), jnp.float32, math.log(0.5), math.log(2.0))), 0.5, 2.0),
        "shift_values": jnp.clip(jnp.exp(jax.random.uniform(seeds[3], (SHIFTS,), jnp.float32, math.log(0.1), math.log(4.0))), 0.1, 4.0),
        "prior_basis": draw_prior_basis(jax.random.fold_in(seeds[5], 71), 0),
    }


LOWER_BOUND = 0.1
UPPER_BOUND = 2.0

def conductances(conduct, padded):
    west_face = 0.5 * (conduct + padded[:-2, 1:-1, 1:-1])
    east_face = 0.5 * (conduct + padded[2:, 1:-1, 1:-1])
    south_face = 0.5 * (conduct + padded[1:-1, :-2, 1:-1])
    north_face = 0.5 * (conduct + padded[1:-1, 2:, 1:-1])
    below_face = 0.5 * (conduct + padded[1:-1, 1:-1, :-2])
    above_face = 0.5 * (conduct + padded[1:-1, 1:-1, 2:])
    return (west_face, east_face, south_face, north_face, below_face, above_face)

def neighbours(padded, face_list):
    west_face, east_face, south_face, north_face, below_face, above_face = face_list
    summed = west_face * padded[..., :-2, 1:-1, 1:-1] + east_face * padded[..., 2:, 1:-1, 1:-1]
    summed = summed + south_face * padded[..., 1:-1, :-2, 1:-1] + north_face * padded[..., 1:-1, 2:, 1:-1]
    summed = summed + below_face * padded[..., 1:-1, 1:-1, :-2] + above_face * padded[..., 1:-1, 1:-1, 2:]
    return summed

def chebyshev(source, face_list, diagonal, padder):
    center = 0.5 * (UPPER_BOUND + LOWER_BOUND)
    spread = 0.5 * (UPPER_BOUND - LOWER_BOUND)
    ratio_value = center / spread
    reciprocal = 1.0 / diagonal
    solution = jnp.zeros_like(source)
    remainder = source
    weight_old = 1.0 / ratio_value
    direction = reciprocal * remainder / center
    for sweep_index in range(SWEEPS):
        solution = solution + direction
        if sweep_index + 1 < SWEEPS:
            applied = diagonal * direction - neighbours(padder(direction), face_list)
            remainder = remainder - applied
            weight_new = 1.0 / (2.0 * ratio_value - weight_old)
            direction = weight_new * weight_old * direction + 2.0 * weight_new / spread * (reciprocal * remainder)
            weight_old = weight_new
    return solution

def products(left_side, right_side):
    return lax.dot_general(left_side, right_side, (((1,), (1,)), ((), ())), precision=lax.Precision.HIGHEST)

def reference(labels, conductance, capacity_table, shift_values, prior_basis):
    conduct = conductance[labels]
    capacity = capacity_table[labels]
    face_list = conductances(conduct, jnp.pad(conduct, 1))
    west_face, east_face, south_face, north_face, below_face, above_face = face_list
    summed = west_face + east_face + (south_face + north_face) + (below_face + above_face)
    diagonal = summed[None, None] + shift_values[:, None, None, None, None] * capacity[None, None]
    tail_columns = prior_basis[BASIS - NEW:].reshape(SHIFTS, COLS, NX, NY, NZ)
    source = tail_columns * capacity[None, None]

    def padder(field):
        return jnp.pad(field, ((0, 0), (0, 0), (1, 1), (1, 1), (1, 1)))
    fields = chebyshev(source, face_list, diagonal, padder)
    cell_weight = 1.0 / (NX * NY * NZ)
    columns = fields.reshape(NEW, NX * NY * NZ)
    flat_basis = prior_basis.reshape(BASIS, NX * NY * NZ)
    first_proj = products(columns, flat_basis) * cell_weight
    columns = columns - jnp.dot(first_proj, flat_basis, precision=lax.Precision.HIGHEST)
    second_proj = products(columns, flat_basis) * cell_weight
    columns = columns - jnp.dot(second_proj, flat_basis, precision=lax.Precision.HIGHEST)
    gram_matrix = products(columns, columns) * cell_weight
    factor = jnp.linalg.cholesky(gram_matrix)
    orthonormal = lax.linalg.triangular_solve(factor, columns, left_side=True, lower=True)
    return (orthonormal.reshape(SHIFTS, COLS, NX, NY, NZ), first_proj + second_proj, factor)
```

```python
import functools

import jax
import jax.numpy as jnp
from jax import lax
from jax.experimental import pallas as pl
from jax.experimental.pallas import tpu as pltpu
from jax.sharding import PartitionSpec as P

COLS = 8
SWEEPS = 4
GROUP = 8
LOWER_BOUND = 0.1
UPPER_BOUND = 2.0
MESH = pl.DeviceIdType.MESH
HIGH = lax.Precision.HIGHEST


def dot_t(a, b):
    return lax.dot_general(
        a, b, (((1,), (1,)), ((), ())), precision=HIGH, preferred_element_type=jnp.float32
    )


def dot(a, b):
    return lax.dot_general(
        a, b, (((1,), (0,)), ((), ())), precision=HIGH, preferred_element_type=jnp.float32
    )


class Reducer:
    def __init__(self, place, src, first, second, full, sems):
        self.place, self.src, self.first, self.second, self.full = place, src, first, second, full
        self.s1, self.r1, self.s2, self.r2, self.s3, self.r3 = sems
        self.chunk = src.shape[0] // GROUP

    def rows(self, t):
        return pl.ds(pl.multiple_of(t * self.chunk, 8), self.chunk)

    def copy1(self, j):
        t = self.place.member(j)
        return pltpu.make_async_remote_copy(
            self.src.at[self.rows(t)], self.first.at[j - 1], self.s1.at[j - 1], self.r1.at[j - 1],
            device_id=self.place.group_id(t), device_id_type=MESH)

    def copy2(self, j, slot, to):
        return pltpu.make_async_remote_copy(
            self.second.at[slot], self.second.at[slot], self.s2.at[j - 1], self.r2.at[slot],
            device_id=self.place.slab_id(to), device_id_type=MESH)

    def copy3(self, j, owner):
        t = self.place.member(j)
        return pltpu.make_async_remote_copy(
            self.full.at[self.rows(owner)], self.full.at[self.rows(owner)],
            self.s3.at[j - 1], self.r3.at[j - 1],
            device_id=self.place.group_id(t), device_id_type=MESH)

    def start1(self):
        for j in range(1, GROUP):
            self.copy1(j).start()

    def start2(self):
        place = self.place
        total = self.src[self.rows(place.g)]
        for j in range(1, GROUP):
            self.copy1(j).wait_recv()
            total = total + self.first[j - 1]
        self.second[place.z] = total
        for j in range(1, place.slabs):
            self.copy2(j, place.z, lax.rem(place.z + j, place.slabs)).start()

    def start3(self):
        place = self.place
        for j in range(1, place.slabs):
            other = lax.rem(place.z + j, place.slabs)
            self.copy2(j, other, other).wait_recv()
        total = self.second[0]
        for i in range(1, place.slabs):
            total = total + self.second[i]
        self.full[self.rows(place.g)] = total
        for j in range(1, GROUP):
            self.copy3(j, place.g).start()

    def finish(self):
        place = self.place
        for j in range(1, GROUP):
            self.copy3(j, place.member(GROUP - j)).wait_recv()
        for j in range(1, GROUP):
            self.copy1(j).wait_send()
            self.copy3(j, place.g).wait_send()
        for j in range(1, place.slabs):
            self.copy2(j, place.z, lax.rem(place.z + j, place.slabs)).wait_send()


class Place:
    def __init__(self, slabs):
        self.s = lax.axis_index("shift")
        self.p = lax.axis_index("space")
        self.b = lax.rem(self.p, 2)
        self.z = self.p // 2
        self.g = self.s * 2 + self.b
        self.slabs = slabs

    def member(self, j):
        return lax.rem(self.g + j, GROUP)

    def group_id(self, t):
        return (t // 2, self.z * 2 + lax.rem(t, 2))

    def slab_id(self, z):
        return (self.s, z * 2 + self.b)


def kernel(slabs, cell_weight, labels_ref, cond_ref, capa_ref, shift_ref, q_ref,
           out_ref, coef_ref, fac_ref,
           lab, kap, cap, face, dg, rc, rem, sol, dirs, wt, qs, ws,
           gsrc, gfirst, gsecond, gfull, psrc, pfirst, psecond, pfull,
           msrc, mfirst, msecond, mfull, aug,
           lab_s, lab_r, in_s, in_r, out_s, out_r, halo_s, halo_r, loc, gsem, psem, msem):
    place = Place(slabs)
    s, b, z, g = place.s, place.b, place.z, place.g
    new = wt.shape[0]
    basis = q_ref.shape[0]
    cells = q_ref.shape[1] * q_ref.shape[2]
    depth = q_ref.shape[3]
    rows_y = lab.shape[1]

    barrier = pltpu.get_barrier_semaphore()
    for j in range(1, GROUP):
        pl.semaphore_signal(barrier, inc=1, device_id=place.group_id(place.member(j)), device_id_type=MESH)
    for j in range(1, slabs):
        pl.semaphore_signal(barrier, inc=1, device_id=place.slab_id(lax.rem(z + j, slabs)), device_id_type=MESH)
    pl.semaphore_wait(barrier, GROUP - 1 + slabs - 1)

    def tail_part(t):
        return q_ref.at[pl.ds(basis - new + t * COLS, COLS)]

    def slot_in(t):
        return rem.at[:, pl.ds(lax.rem(t, 2) * 2, 2), pl.ds(pl.multiple_of((t // 2) * 8, 8), 8), :]

    def copy_in(j, to, owner):
        return pltpu.make_async_remote_copy(
            tail_part(to), slot_in(owner), in_s.at[j - 1], in_r.at[j - 1],
            device_id=place.group_id(to), device_id_type=MESH)

    pair = lax.rem(b + 1, 2)
    own = lab.at[pl.ds(1 + 2 * b, 2)]
    lab[pl.ds(1 + 2 * b, 2)] = labels_ref[...]
    lab_pair = pltpu.make_async_remote_copy(
        labels_ref, own, lab_s.at[0], lab_r.at[0], device_id=(s, z * 2 + pair), device_id_type=MESH)
    lab_pair.start()

    def edge(ref_src, dst_plane, k, to):
        return pltpu.make_async_remote_copy(
            lab.at[ref_src], lab.at[dst_plane], lab_s.at[k], lab_r.at[k],
            device_id=place.slab_id(to), device_id_type=MESH)

    for j in range(1, GROUP):
        copy_in(j, place.member(j), g).start()
    mine = pltpu.make_async_copy(tail_part(g), slot_in(g), loc.at[0])
    mine.start()

    gsrc[...] = jnp.zeros_like(gsrc)
    for k in range(cells):
        block = q_ref[:, k // 8, k % 8, :]
        qs[k] = block
    @pl.loop(0, cells)
    def _(k):
        block = qs[k]
        gsrc[...] += dot_t(block, block)

    pltpu.make_async_remote_copy(
        labels_ref, lab.at[pl.ds(1 + 2 * pair, 2)], lab_s.at[0], lab_r.at[0],
        device_id=(s, z * 2 + pair), device_id_type=MESH).wait_recv()

    @pl.when(z > 0)
    def _():
        edge(1, 5, 1, z - 1).start()

    @pl.when(z < slabs - 1)
    def _():
        edge(4, 0, 2, z + 1).start()

    @pl.when(z == 0)
    def _():
        lab[0] = jnp.full((rows_y, depth), -1, jnp.int32)
        for n in range(SWEEPS - 1):
            dirs[n, :, 0] = jnp.zeros((COLS, rows_y, depth), jnp.float32)

    @pl.when(z == slabs - 1)
    def _():
        lab[5] = jnp.full((rows_y, depth), -1, jnp.int32)
        for n in range(SWEEPS - 1):
            dirs[n, :, 5] = jnp.zeros((COLS, rows_y, depth), jnp.float32)

    @pl.when(z > 0)
    def _():
        edge(4, 0, 2, z - 1).wait_recv()

    @pl.when(z < slabs - 1)
    def _():
        edge(1, 5, 1, z + 1).wait_recv()

    @pl.loop(0, 6)
    def _(i):
        value = lab[i]
        k_acc = jnp.zeros((rows_y, depth), jnp.float32)
        for m in range(cond_ref.shape[0]):
            k_acc = jnp.where(value == m, cond_ref[m], k_acc)
        kap[i] = k_acc

    shift = shift_ref[g]
    row = lax.broadcasted_iota(jnp.int32, (rows_y, depth), 0)
    lane = lax.broadcasted_iota(jnp.int32, (rows_y, depth), 1)

    @pl.loop(0, 4)
    def _(i):
        value = lab[i + 1]
        c_acc = jnp.zeros((rows_y, depth), jnp.float32)
        for m in range(capa_ref.shape[0]):
            c_acc = jnp.where(value == m, capa_ref[m], c_acc)
        cap[i] = c_acc
        me = kap[i + 1]
        west = 0.5 * (me + kap[i])
        east = 0.5 * (me + kap[i + 2])
        zero = jnp.zeros_like(me)
        k_south = jnp.where(row == 0, zero, pltpu.roll(me, 1, 0))
        k_north = jnp.where(row == rows_y - 1, zero, pltpu.roll(me, rows_y - 1, 0))
        k_below = jnp.where(lane == 0, zero, pltpu.roll(me, 1, 1))
        k_above = jnp.where(lane == depth - 1, zero, pltpu.roll(me, depth - 1, 1))
        south = 0.5 * (me + k_south)
        north = 0.5 * (me + k_north)
        below = 0.5 * (me + k_below)
        above = 0.5 * (me + k_above)
        diag = ((west + east) + (south + north)) + (below + above) + shift * c_acc
        dg[i] = diag
        rc[i] = 1.0 / diag
        face[0, i] = west
        face[1, i] = east
        face[2, i] = jnp.where(row == 0, zero, south)
        face[3, i] = jnp.where(row == rows_y - 1, zero, north)
        face[4, i] = jnp.where(lane == 0, zero, below)
        face[5, i] = jnp.where(lane == depth - 1, zero, above)

    greduce = Reducer(place, gsrc, gfirst, gsecond, gfull, [gsem.at[i] for i in range(6)])

    mine.wait()
    for j in range(1, GROUP):
        copy_in(j, place.member(j), place.member(GROUP - j)).wait_recv()
    greduce.start1()

    center = 0.5 * (UPPER_BOUND + LOWER_BOUND)
    spread = 0.5 * (UPPER_BOUND - LOWER_BOUND)
    ratio = center / spread

    @pl.loop(0, 4)
    def _(i):
        @pl.loop(0, COLS)
        def _(c):
            r = rem[c, i] * cap[i]
            d = (rc[i] * r) / center
            rem[c, i] = r
            sol[c, i] = d
            dirs[0, c, i + 1] = d

    def halo(n, src, dst, k, to):
        return pltpu.make_async_remote_copy(
            dirs.at[n, :, src], dirs.at[n, :, dst], halo_s.at[n, k], halo_r.at[n, k],
            device_id=place.slab_id(to), device_id_type=MESH)

    weight_old = 1.0 / ratio
    for n in range(SWEEPS - 1):
        @pl.when(z > 0)
        def _():
            halo(n, 1, 5, 0, z - 1).start()

        @pl.when(z < slabs - 1)
        def _():
            halo(n, 4, 0, 1, z + 1).start()

        if n == 0:
            greduce.start2()
        if n == 1:
            greduce.start3()
        if n == 2:
            greduce.finish()

        @pl.when(z > 0)
        def _():
            halo(n, 4, 0, 1, z - 1).wait_recv()

        @pl.when(z < slabs - 1)
        def _():
            halo(n, 1, 5, 0, z + 1).wait_recv()

        weight = 1.0 / (2.0 * ratio - weight_old)
        keep, step = weight * weight_old, 2.0 * weight / spread
        weight_old = weight

        @pl.loop(0, 4)
        def _(i):
            @pl.loop(0, COLS)
            def _(c):
                d = dirs[n, c, i + 1]
                near = face[0, i] * dirs[n, c, i] + face[1, i] * dirs[n, c, i + 2]
                near = near + face[2, i] * pltpu.roll(d, 1, 0) + face[3, i] * pltpu.roll(d, rows_y - 1, 0)
                near = near + face[4, i] * pltpu.roll(d, 1, 1) + face[5, i] * pltpu.roll(d, depth - 1, 1)
                r = rem[c, i] - (dg[i] * d - near)
                nd = keep * d + step * (rc[i] * r)
                sol[c, i] = sol[c, i] + nd
                if n + 1 < SWEEPS - 1:
                    rem[c, i] = r
                    dirs[n + 1, c, i + 1] = nd

    def slot_out(t):
        return sol.at[:, pl.ds(lax.rem(t, 2) * 2, 2), pl.ds(pl.multiple_of((t // 2) * 8, 8), 8), :]

    def copy_out(j, to, owner):
        return pltpu.make_async_remote_copy(
            slot_out(to), wt.at[pl.ds(owner * COLS, COLS)], out_s.at[j - 1], out_r.at[j - 1],
            device_id=place.group_id(to), device_id_type=MESH)

    for j in range(1, GROUP):
        copy_out(j, place.member(j), g).start()
    back = pltpu.make_async_copy(slot_out(g), wt.at[pl.ds(g * COLS, COLS)], loc.at[1])
    back.start()

    lab_pair.wait_send()

    @pl.when(z > 0)
    def _():
        edge(1, 5, 1, z - 1).wait_send()
        for n in range(SWEEPS - 1):
            halo(n, 1, 5, 0, z - 1).wait_send()

    @pl.when(z < slabs - 1)
    def _():
        edge(4, 0, 2, z + 1).wait_send()
        for n in range(SWEEPS - 1):
            halo(n, 4, 0, 1, z + 1).wait_send()

    for j in range(1, GROUP):
        copy_in(j, place.member(j), g).wait_send()

    back.wait()
    for j in range(1, GROUP):
        copy_out(j, place.member(j), place.member(GROUP - j)).wait_recv()

    for k in range(cells):
        ws[k] = wt[:, k // 8, k % 8, :]
    psrc[...] = jnp.zeros_like(psrc)
    @pl.loop(0, cells)
    def _(k):
        psrc[...] += dot_t(ws[k], qs[k])
    preduce = Reducer(place, psrc, pfirst, psecond, pfull, [psem.at[i] for i in range(6)])
    preduce.start1()
    preduce.start2()
    preduce.start3()
    for j in range(1, GROUP):
        copy_out(j, place.member(j), g).wait_send()
    preduce.finish()

    proj = pfull[...] * cell_weight
    coef = proj + (proj - dot(proj, gfull[...] * cell_weight))
    coef_ref[...] = coef
    msrc[...] = jnp.zeros_like(msrc)
    @pl.loop(0, cells)
    def _(k):
        w2 = ws[k] - dot(coef_ref[...], qs[k])
        ws[k] = w2
        msrc[...] += dot_t(w2, w2)
    mreduce = Reducer(place, msrc, mfirst, msecond, mfull, [msem.at[i] for i in range(6)])
    mreduce.start1()
    mreduce.start2()
    mreduce.start3()
    mreduce.finish()

    gram = mfull[...] * cell_weight
    r64 = lax.broadcasted_iota(jnp.int32, (new, new), 0)
    c64 = lax.broadcasted_iota(jnp.int32, (new, new), 1)
    eye = jnp.where(r64 == c64, 1.0, 0.0).astype(jnp.float32)
    work = jnp.concatenate([gram, eye], axis=1)
    for j in range(new - 1):
        lo = (j // 8) * 8
        live = work[lo:]
        pivot_row = work[j:j + 1]
        scaled = pivot_row / pivot_row[:, j:j + 1]
        col = live[:, j:j + 1]
        below_pivot = lax.broadcasted_iota(jnp.int32, (new - lo, 1), 0) > (j - lo)
        live = live - jnp.where(below_pivot, col, 0.0) * scaled
        work = jnp.concatenate([work[:lo], live], axis=0) if lo else live
    diag = jnp.sum(jnp.where(r64 == c64, work[:, :new], 0.0), axis=1, keepdims=True)
    work = work / jnp.sqrt(diag)
    upper = jnp.where(c64 >= r64, work[:, :new], 0.0)
    fac_ref[...] = lax.dot_general(
        upper, eye, (((0,), (0,)), ((), ())), precision=HIGH, preferred_element_type=jnp.float32)
    aug[...] = work[:, new:]
    @pl.loop(0, cells)
    def _(k):
        ws[k] = dot(aug[...], ws[k])
    for k in range(cells):
        out_ref[:, k // 8, k % 8, :] = ws[k]


def local(slabs, labels, conductance, capacity_table, shift_values, prior_basis):
    basis, slab_x, quarter, depth = prior_basis.shape
    shifts = shift_values.shape[0]
    new = shifts * COLS
    rows_y = labels.shape[1]
    cells = slab_x * quarter
    count = cells * depth * lax.axis_size("shift") * lax.axis_size("space")
    f32 = jnp.float32

    def reducer(rows, lanes):
        c = rows // GROUP
        return [pltpu.VMEM((rows, lanes), f32), pltpu.VMEM((GROUP - 1, c, lanes), f32),
                pltpu.VMEM((slabs, c, lanes), f32), pltpu.VMEM((rows, lanes), f32)]

    dma = pltpu.SemaphoreType.DMA
    width = max(GROUP, slabs)
    vmem = pl.BlockSpec(memory_space=pltpu.VMEM)
    smem = pl.BlockSpec(memory_space=pltpu.SMEM)
    block, coef, factor = pl.pallas_call(
        functools.partial(kernel, slabs, 1.0 / count),
        out_shape=[
            jax.ShapeDtypeStruct((new, slab_x, quarter, depth), f32),
            jax.ShapeDtypeStruct((new, basis), f32),
            jax.ShapeDtypeStruct((new, new), f32),
        ],
        in_specs=[vmem, smem, smem, smem, vmem],
        out_specs=[vmem] * 3,
        scratch_shapes=[
            pltpu.VMEM((6, rows_y, depth), jnp.int32),
            pltpu.VMEM((6, rows_y, depth), f32),
            pltpu.VMEM((4, rows_y, depth), f32),
            pltpu.VMEM((6, 4, rows_y, depth), f32),
            pltpu.VMEM((4, rows_y, depth), f32),
            pltpu.VMEM((4, rows_y, depth), f32),
            pltpu.VMEM((COLS, 4, rows_y, depth), f32),
            pltpu.VMEM((COLS, 4, rows_y, depth), f32),
            pltpu.VMEM((SWEEPS - 1, COLS, 6, rows_y, depth), f32),
            pltpu.VMEM((new, slab_x, quarter, depth), f32),
            pltpu.VMEM((cells, basis, depth), f32),
            pltpu.VMEM((cells, new, depth), f32),
            *reducer(basis, basis),
            *reducer(new, basis),
            *reducer(new, new),
            pltpu.VMEM((new, new), f32),
            dma((3,)), dma((3,)), dma((GROUP - 1,)), dma((GROUP - 1,)),
            dma((GROUP - 1,)), dma((GROUP - 1,)), dma((SWEEPS - 1, 2)), dma((SWEEPS - 1, 2)),
            dma((2,)), dma((6, width)), dma((6, width)), dma((6, width)),
        ],
        compiler_params=pltpu.CompilerParams(
            collective_id=0, has_side_effects=True, vmem_limit_bytes=48 * 1024 * 1024),
    )(labels, conductance, capacity_table, shift_values, prior_basis)
    return block.reshape(shifts, COLS, slab_x, quarter, depth), coef, factor


def solution(mesh):
    in_specs = (P("space", None, None), P(), P(), P(), P(None, "space", "shift", None))
    out_specs = (P(None, None, "space", "shift", None), P(), P())
    slabs = mesh.shape["space"] // 2
    return jax.shard_map(
        functools.partial(local, slabs), mesh=mesh, in_specs=in_specs, out_specs=out_specs, check_vma=False)
```

```python
import functools

import jax
import jax.numpy as jnp
from jax import lax
from jax.experimental import pallas as pl
from jax.experimental.pallas import tpu as pltpu
from jax.sharding import PartitionSpec as P

COLS = 8
SWEEPS = 4
GROUP = 8
LOWER_BOUND = 0.1
UPPER_BOUND = 2.0
MESH = pl.DeviceIdType.MESH
HIGH = lax.Precision.HIGHEST


def dot(a, b):
    return lax.dot_general(
        a, b, (((1,), (0,)), ((), ())), precision=HIGH, preferred_element_type=jnp.float32
    )


class Reducer:
    def __init__(self, place, src, first, second, full, sems):
        self.place, self.src, self.first, self.second, self.full = place, src, first, second, full
        self.s1, self.r1, self.s2, self.r2, self.s3, self.r3 = sems
        self.chunk = src.shape[0] // GROUP

    def rows(self, t):
        return pl.ds(pl.multiple_of(t * self.chunk, 8), self.chunk)

    def copy1(self, j):
        t = self.place.member(j)
        return pltpu.make_async_remote_copy(
            self.src.at[self.rows(t)], self.first.at[j - 1], self.s1.at[j - 1], self.r1.at[j - 1],
            device_id=self.place.group_id(t), device_id_type=MESH)

    def copy2(self, j, slot, to):
        return pltpu.make_async_remote_copy(
            self.second.at[slot], self.second.at[slot], self.s2.at[j - 1], self.r2.at[slot],
            device_id=self.place.slab_id(to), device_id_type=MESH)

    def copy3(self, j, owner):
        t = self.place.member(j)
        return pltpu.make_async_remote_copy(
            self.full.at[self.rows(owner)], self.full.at[self.rows(owner)],
            self.s3.at[j - 1], self.r3.at[j - 1],
            device_id=self.place.group_id(t), device_id_type=MESH)

    def start1(self):
        for j in range(1, GROUP):
            self.copy1(j).start()

    def start2(self):
        place = self.place
        total = self.src[self.rows(place.g)]
        for j in range(1, GROUP):
            self.copy1(j).wait_recv()
            total = total + self.first[j - 1]
        self.second[place.z] = total
        for j in range(1, place.slabs):
            self.copy2(j, place.z, lax.rem(place.z + j, place.slabs)).start()

    def start3(self):
        place = self.place
        for j in range(1, place.slabs):
            other = lax.rem(place.z + j, place.slabs)
            self.copy2(j, other, other).wait_recv()
        total = self.second[0]
        for i in range(1, place.slabs):
            total = total + self.second[i]
        self.full[self.rows(place.g)] = total
        for j in range(1, GROUP):
            self.copy3(j, place.g).start()

    def finish(self):
        place = self.place
        for j in range(1, GROUP):
            self.copy3(j, place.member(GROUP - j)).wait_recv()
        for j in range(1, GROUP):
            self.copy1(j).wait_send()
            self.copy3(j, place.g).wait_send()
        for j in range(1, place.slabs):
            self.copy2(j, place.z, lax.rem(place.z + j, place.slabs)).wait_send()


class Place:
    def __init__(self, slabs):
        self.s = lax.axis_index("shift")
        self.p = lax.axis_index("space")
        self.b = lax.rem(self.p, 2)
        self.z = self.p // 2
        self.g = self.s * 2 + self.b
        self.slabs = slabs

    def member(self, j):
        return lax.rem(self.g + j, GROUP)

    def group_id(self, t):
        return (t // 2, self.z * 2 + lax.rem(t, 2))

    def slab_id(self, z):
        return (self.s, z * 2 + self.b)


def split(x):
    hi = x.astype(jnp.bfloat16)
    return hi, (x - hi.astype(jnp.float32)).astype(jnp.bfloat16)


def raw(a, b, dims):
    return lax.dot_general(a, b, (dims, ((), ())), preferred_element_type=jnp.float32)


def dot3(a_hi, a_lo, b_hi, b_lo, dims):
    rows = a_hi.shape[0]
    both = raw(jnp.concatenate([a_hi, a_lo], axis=0), b_hi, dims)
    return both[:rows] + (both[rows:] + raw(a_hi, b_lo, dims))


TRANSPOSED = ((1,), (1,))
PLAIN = ((1,), (0,))


def kernel(slabs, cell_weight, labels_hbm, cond_hbm, capa_hbm, shift_hbm, q_hbm,
           out_hbm, coef_ref, fac_ref,
           lab, kap, cap, face, dg, rc, rem, sol, dirs, wt, qs, qh, ql, wh, wl,
           gsrc, gfirst, gsecond, gfull, psrc, pfirst, psecond, pfull,
           msrc, mfirst, msecond, mfull, cross, cond_ref, capa_ref, shift_ref,
           lab_s, lab_r, in_s, in_r, out_s, out_r, halo_s, halo_r, loc, qsem, osem, gsem, psem, msem):
    place = Place(slabs)
    s, b, z, g = place.s, place.b, place.z, place.g
    f32 = jnp.float32
    basis, slab_x, quarter, depth = q_hbm.shape
    new = wt.shape[2]
    cells = slab_x * quarter
    rows_y = lab.shape[1]
    old = basis - new

    def load(k, first, count, i):
        return pltpu.make_async_copy(
            q_hbm.at[pl.ds(first, count), k // quarter, k % quarter, :],
            qs.at[k // quarter, k % quarter, pl.ds(first, count), :], qsem.at[i, k])

    for k in range(cells):
        load(k, old, new, 0).start()
    own_lab = pltpu.make_async_copy(labels_hbm, lab.at[pl.ds(1 + 2 * b, 2)], loc.at[2])
    own_lab.start()
    tables = [pltpu.make_async_copy(src, dst, loc.at[3 + i]) for i, (src, dst) in enumerate(
        [(cond_hbm, cond_ref), (capa_hbm, capa_ref), (shift_hbm, shift_ref)])]
    for copy in tables:
        copy.start()
    for k in range(cells):
        load(k, 0, old, 1).start()

    barrier = pltpu.get_barrier_semaphore()
    for j in range(1, GROUP):
        pl.semaphore_signal(barrier, inc=1, device_id=place.group_id(place.member(j)), device_id_type=MESH)
    for j in range(1, slabs):
        pl.semaphore_signal(barrier, inc=1, device_id=place.slab_id(lax.rem(z + j, slabs)), device_id_type=MESH)
    for n in range(SWEEPS - 1):
        for i in range(1, 5):
            dirs[n, i, 0] = jnp.zeros((COLS, depth), f32)
            dirs[n, i, rows_y + 1] = jnp.zeros((COLS, depth), f32)
    pl.semaphore_wait(barrier, GROUP - 1 + slabs - 1)

    pair = lax.rem(b + 1, 2)

    def lab_pair(owner):
        return pltpu.make_async_remote_copy(
            labels_hbm, lab.at[pl.ds(1 + 2 * owner, 2)], lab_s.at[0], lab_r.at[0],
            device_id=(s, z * 2 + pair), device_id_type=MESH)

    def edge(from_plane, to_plane, k, to):
        return pltpu.make_async_remote_copy(
            lab.at[from_plane], lab.at[to_plane], lab_s.at[k], lab_r.at[k],
            device_id=place.slab_id(to), device_id_type=MESH)

    def slot(field, t):
        return field.at[pl.ds(lax.rem(t, 2) * 2, 2), pl.ds((t // 2) * quarter, quarter)]

    def copy_in(j, to, owner):
        return pltpu.make_async_remote_copy(
            qs.at[:, :, pl.ds(pl.multiple_of(old + to * COLS, COLS), COLS), :], slot(rem, owner),
            in_s.at[j - 1], in_r.at[j - 1], device_id=place.group_id(to), device_id_type=MESH)

    lab_pair(b).start()
    for k in range(cells):
        load(k, old, new, 0).wait()
    for j in range(1, GROUP):
        copy_in(j, place.member(j), g).start()
    mine = pltpu.make_async_copy(
        qs.at[:, :, pl.ds(pl.multiple_of(old + g * COLS, COLS), COLS), :], slot(rem, g), loc.at[0])
    mine.start()
    own_lab.wait()
    lab_pair(pair).wait_recv()

    @pl.when(z > 0)
    def _():
        edge(1, 5, 1, z - 1).start()

    @pl.when(z < slabs - 1)
    def _():
        edge(4, 0, 2, z + 1).start()

    for end, there in ((0, z == 0), (5, z == slabs - 1)):
        @pl.when(there)
        def _():
            lab[end] = jnp.full((rows_y, depth), -1, jnp.int32)
            for n in range(SWEEPS - 1):
                dirs[n, end] = jnp.zeros((rows_y + 2, COLS, depth), f32)

    for k in range(cells):
        load(k, 0, old, 1).wait()
    gsrc[...] = jnp.zeros_like(gsrc)
    cross[...] = jnp.zeros_like(cross)

    @pl.loop(0, cells)
    def _(k):
        hi, lo = split(qs[k // quarter, lax.rem(k, quarter)])
        qh[k] = hi
        ql[k] = lo
        gsrc[...] += raw(hi, hi, TRANSPOSED)
        cross[...] += raw(hi, lo, TRANSPOSED)

    gsrc[...] += cross[...] + cross[...].T

    @pl.when(z > 0)
    def _():
        edge(4, 0, 2, z - 1).wait_recv()

    @pl.when(z < slabs - 1)
    def _():
        edge(1, 5, 1, z + 1).wait_recv()

    for copy in tables:
        copy.wait()

    @pl.loop(0, 6)
    def _(i):
        value = lab[i]
        k_acc = jnp.zeros((rows_y, depth), f32)
        for m in range(cond_ref.shape[0]):
            k_acc = jnp.where(value == m, cond_ref[m], k_acc)
        kap[i] = k_acc

    shift = shift_ref[g]
    row = lax.broadcasted_iota(jnp.int32, (rows_y, depth), 0)
    lane = lax.broadcasted_iota(jnp.int32, (rows_y, depth), 1)

    @pl.loop(0, 4)
    def _(i):
        value = lab[i + 1]
        c_acc = jnp.zeros((rows_y, depth), f32)
        for m in range(capa_ref.shape[0]):
            c_acc = jnp.where(value == m, capa_ref[m], c_acc)
        cap[i] = c_acc
        me = kap[i + 1]
        zero = jnp.zeros_like(me)
        west = 0.5 * (me + kap[i])
        east = 0.5 * (me + kap[i + 2])
        south = 0.5 * (me + jnp.where(row == 0, zero, pltpu.roll(me, 1, 0)))
        north = 0.5 * (me + jnp.where(row == rows_y - 1, zero, pltpu.roll(me, rows_y - 1, 0)))
        below = 0.5 * (me + jnp.where(lane == 0, zero, pltpu.roll(me, 1, 1)))
        above = 0.5 * (me + jnp.where(lane == depth - 1, zero, pltpu.roll(me, depth - 1, 1)))
        diag = ((west + east) + (south + north)) + (below + above) + shift * c_acc
        dg[i] = diag
        rc[i] = 1.0 / diag
        face[0, i] = west
        face[1, i] = east
        face[2, i] = south
        face[3, i] = north
        face[4, i] = jnp.where(lane == 0, zero, below)
        face[5, i] = jnp.where(lane == depth - 1, zero, above)

    greduce = Reducer(place, gsrc, gfirst, gsecond, gfull, [gsem.at[i] for i in range(6)])

    mine.wait()
    for j in range(1, GROUP):
        copy_in(j, place.member(j), place.member(GROUP - j)).wait_recv()
    greduce.start1()

    center = 0.5 * (UPPER_BOUND + LOWER_BOUND)
    spread = 0.5 * (UPPER_BOUND - LOWER_BOUND)
    ratio = center / spread

    def begin(i):
        @pl.loop(0, rows_y // 8)
        def _(t):
            tile = pl.ds(pl.multiple_of(t * 8, 8), 8)
            c_t, rc_t = cap[i, tile], rc[i, tile]
            for u in range(8):
                y = t * 8 + u
                r = rem[i, y] * c_t[u:u + 1]
                d = (rc_t[u:u + 1] * r) / center
                rem[i, y] = r
                sol[i, y] = d
                dirs[0, i + 1, y + 1] = d

    def sweep(n, i, keep, step):
        @pl.loop(0, rows_y // 8)
        def _(t):
            tile = pl.ds(pl.multiple_of(t * 8, 8), 8)
            f = [face[k, i, tile] for k in range(6)]
            dg_t, rc_t = dg[i, tile], rc[i, tile]
            for u in range(8):
                y = t * 8 + u
                w_, e_, s_, n_, b_, a_ = [v[u:u + 1] for v in f]
                d = dirs[n, i + 1, y + 1]
                near = w_ * dirs[n, i, y + 1] + e_ * dirs[n, i + 2, y + 1]
                near = near + s_ * dirs[n, i + 1, y] + n_ * dirs[n, i + 1, y + 2]
                near = near + b_ * pltpu.roll(d, 1, 1) + a_ * pltpu.roll(d, depth - 1, 1)
                r = rem[i, y] - (dg_t[u:u + 1] * d - near)
                nd = keep * d + step * (rc_t[u:u + 1] * r)
                sol[i, y] = sol[i, y] + nd
                if n + 1 < SWEEPS - 1:
                    rem[i, y] = r
                    dirs[n + 1, i + 1, y + 1] = nd

    def halo(n, src, dst, k, to):
        return pltpu.make_async_remote_copy(
            dirs.at[n, src, pl.ds(1, rows_y)], dirs.at[n, dst, pl.ds(1, rows_y)],
            halo_s.at[n, k], halo_r.at[n, k], device_id=place.slab_id(to), device_id_type=MESH)

    def send_halo(n):
        @pl.when(z > 0)
        def _():
            halo(n, 1, 5, 0, z - 1).start()

        @pl.when(z < slabs - 1)
        def _():
            halo(n, 4, 0, 1, z + 1).start()

    begin(0)
    begin(3)
    send_halo(0)
    begin(1)
    begin(2)
    weight_old = 1.0 / ratio
    for n in range(SWEEPS - 1):
        weight = 1.0 / (2.0 * ratio - weight_old)
        keep, step = weight * weight_old, 2.0 * weight / spread
        weight_old = weight
        sweep(n, 1, keep, step)
        sweep(n, 2, keep, step)
        if n == 0:
            greduce.start2()
        if n == 1:
            greduce.start3()
        if n == 2:
            greduce.finish()

        @pl.when(z > 0)
        def _():
            halo(n, 4, 0, 1, z - 1).wait_recv()

        @pl.when(z < slabs - 1)
        def _():
            halo(n, 1, 5, 0, z + 1).wait_recv()

        sweep(n, 0, keep, step)
        sweep(n, 3, keep, step)
        if n + 1 < SWEEPS - 1:
            send_halo(n + 1)

    def copy_out(j, to, owner):
        return pltpu.make_async_remote_copy(
            slot(sol, to), wt.at[:, :, pl.ds(pl.multiple_of(owner * COLS, COLS), COLS), :],
            out_s.at[j - 1], out_r.at[j - 1], device_id=place.group_id(to), device_id_type=MESH)

    for j in range(1, GROUP):
        copy_out(j, place.member(j), g).start()
    back = pltpu.make_async_copy(
        slot(sol, g), wt.at[:, :, pl.ds(pl.multiple_of(g * COLS, COLS), COLS), :], loc.at[1])
    back.start()

    lab_pair(b).wait_send()

    @pl.when(z > 0)
    def _():
        edge(1, 5, 1, z - 1).wait_send()
        for n in range(SWEEPS - 1):
            halo(n, 1, 5, 0, z - 1).wait_send()

    @pl.when(z < slabs - 1)
    def _():
        edge(4, 0, 2, z + 1).wait_send()
        for n in range(SWEEPS - 1):
            halo(n, 4, 0, 1, z + 1).wait_send()

    for j in range(1, GROUP):
        copy_in(j, place.member(j), g).wait_send()
    psrc[...] = jnp.zeros_like(psrc)
    msrc[...] = jnp.zeros_like(msrc)
    back.wait()
    for j in range(1, GROUP):
        copy_out(j, place.member(j), place.member(GROUP - j)).wait_recv()

    @pl.loop(0, cells // 4)
    def _(k4):
        total = psrc[...]
        for i in range(4):
            k = k4 * 4 + i
            hi, lo = split(wt[k // quarter, lax.rem(k, quarter)])
            total = total + dot3(hi, lo, qh[k], ql[k], TRANSPOSED)
        psrc[...] = total

    preduce = Reducer(place, psrc, pfirst, psecond, pfull, [psem.at[i] for i in range(6)])
    preduce.start1()
    preduce.start2()
    preduce.start3()
    for j in range(1, GROUP):
        copy_out(j, place.member(j), g).wait_send()
    preduce.finish()

    proj = pfull[...] * cell_weight
    coef = proj + (proj - dot(proj, gfull[...] * cell_weight))
    coef_ref[...] = coef
    coef_hi, coef_lo = split(coef)
    qs_new = pl.ds(0, new)

    @pl.loop(0, cells // 4)
    def _(k4):
        same = msrc[...]
        mixed = cross[qs_new, qs_new] * jnp.where(k4 == 0, 0.0, 1.0)
        for i in range(4):
            k = k4 * 4 + i
            w2 = wt[k // quarter, lax.rem(k, quarter)] - dot3(coef_hi, coef_lo, qh[k], ql[k], PLAIN)
            hi, lo = split(w2)
            wh[k] = hi
            wl[k] = lo
            same = same + raw(hi, hi, TRANSPOSED)
            mixed = mixed + raw(hi, lo, TRANSPOSED)
        msrc[...] = same
        cross[qs_new, qs_new] = mixed

    mixed = cross[qs_new, qs_new]
    msrc[...] += mixed + mixed.T
    mreduce = Reducer(place, msrc, mfirst, msecond, mfull, [msem.at[i] for i in range(6)])
    mreduce.start1()
    mreduce.start2()
    mreduce.start3()
    mreduce.finish()

    gram = mfull[...] * cell_weight
    r64 = lax.broadcasted_iota(jnp.int32, (new, new), 0)
    c64 = lax.broadcasted_iota(jnp.int32, (new, new), 1)
    eye = jnp.where(r64 == c64, 1.0, 0.0).astype(f32)
    work = jnp.concatenate([gram, eye], axis=1)
    for j in range(new - 1):
        lo = (j // 8) * 8
        live = work[lo:]
        pivot_row = work[j:j + 1]
        scaled = pivot_row / pivot_row[:, j:j + 1]
        col = live[:, j:j + 1]
        below_pivot = lax.broadcasted_iota(jnp.int32, (new - lo, 1), 0) > (j - lo)
        live = live - jnp.where(below_pivot, col, 0.0) * scaled
        work = jnp.concatenate([work[:lo], live], axis=0) if lo else live
    diag = jnp.sum(jnp.where(r64 == c64, work[:, :new], 0.0), axis=1, keepdims=True)
    work = work / jnp.sqrt(diag)
    upper = jnp.where(c64 >= r64, work[:, :new], 0.0)
    fac_ref[...] = lax.dot_general(
        upper, eye, (((0,), (0,)), ((), ())), precision=HIGH, preferred_element_type=f32)
    inv_hi, inv_lo = split(work[:, new:])

    def result(k):
        return pltpu.make_async_copy(
            wt.at[k // quarter, k % quarter], out_hbm.at[:, k // quarter, k % quarter, :], osem.at[k])

    for k in range(cells):
        wt[k // quarter, k % quarter] = dot3(inv_hi, inv_lo, wh[k], wl[k], PLAIN)
        result(k).start()
    for k in range(cells):
        result(k).wait()


def local(slabs, labels, conductance, capacity_table, shift_values, prior_basis):
    basis, slab_x, quarter, depth = prior_basis.shape
    shifts = shift_values.shape[0]
    new = shifts * COLS
    rows_y = labels.shape[1]
    cells = slab_x * quarter
    count = cells * depth * lax.axis_size("shift") * lax.axis_size("space")
    f32 = jnp.float32

    def reducer(rows, lanes):
        c = rows // GROUP
        return [pltpu.VMEM((rows, lanes), f32), pltpu.VMEM((GROUP - 1, c, lanes), f32),
                pltpu.VMEM((slabs, c, lanes), f32), pltpu.VMEM((rows, lanes), f32)]

    dma = pltpu.SemaphoreType.DMA
    width = max(GROUP, slabs)
    vmem = pl.BlockSpec(memory_space=pltpu.VMEM)
    block, coef, factor = pl.pallas_call(
        functools.partial(kernel, slabs, 1.0 / count),
        out_shape=[
            jax.ShapeDtypeStruct((new, slab_x, quarter, depth), f32),
            jax.ShapeDtypeStruct((new, basis), f32),
            jax.ShapeDtypeStruct((new, new), f32),
        ],
        in_specs=[pl.BlockSpec(memory_space=pl.ANY)] * 5,
        out_specs=[pl.BlockSpec(memory_space=pl.ANY), vmem, vmem],
        scratch_shapes=[
            pltpu.VMEM((6, rows_y, depth), jnp.int32),
            pltpu.VMEM((6, rows_y, depth), f32),
            pltpu.VMEM((4, rows_y, depth), f32),
            pltpu.VMEM((6, 4, rows_y, depth), f32),
            pltpu.VMEM((4, rows_y, depth), f32),
            pltpu.VMEM((4, rows_y, depth), f32),
            pltpu.VMEM((4, rows_y, COLS, depth), f32),
            pltpu.VMEM((4, rows_y, COLS, depth), f32),
            pltpu.VMEM((SWEEPS - 1, 6, rows_y + 2, COLS, depth), f32),
            pltpu.VMEM((slab_x, quarter, new, depth), f32),
            pltpu.VMEM((slab_x, quarter, basis, depth), f32),
            pltpu.VMEM((cells, basis, depth), jnp.bfloat16),
            pltpu.VMEM((cells, basis, depth), jnp.bfloat16),
            pltpu.VMEM((cells, new, depth), jnp.bfloat16),
            pltpu.VMEM((cells, new, depth), jnp.bfloat16),
            *reducer(basis, basis),
            *reducer(new, basis),
            *reducer(new, new),
            pltpu.VMEM((basis, basis), f32),
            pltpu.SMEM(conductance.shape, f32),
            pltpu.SMEM(capacity_table.shape, f32),
            pltpu.SMEM(shift_values.shape, f32),
            dma((3,)), dma((3,)), dma((GROUP - 1,)), dma((GROUP - 1,)),
            dma((GROUP - 1,)), dma((GROUP - 1,)), dma((SWEEPS - 1, 2)), dma((SWEEPS - 1, 2)),
            dma((6,)), dma((2, cells)), dma((cells,)),
            dma((6, width)), dma((6, width)), dma((6, width)),
        ],
        compiler_params=pltpu.CompilerParams(
            collective_id=0, has_side_effects=True, vmem_limit_bytes=48 * 1024 * 1024),
    )(labels, conductance, capacity_table, shift_values, prior_basis)
    return block.reshape(shifts, COLS, slab_x, quarter, depth), coef, factor


def solution(mesh):
    in_specs = (P("space", None, None), P(), P(), P(), P(None, "space", "shift", None))
    out_specs = (P(None, None, "space", "shift", None), P(), P())
    slabs = mesh.shape["space"] // 2
    return jax.shard_map(
        functools.partial(local, slabs), mesh=mesh, in_specs=in_specs, out_specs=out_specs, check_vma=False)
```

```python
import functools

import jax
import jax.numpy as jnp
from jax import lax
from jax.experimental import pallas as pl
from jax.experimental.pallas import tpu as pltpu
from jax.sharding import PartitionSpec as P

COLS = 8
SWEEPS = 4
GROUP = 8
LOWER_BOUND = 0.1
UPPER_BOUND = 2.0
MESH = pl.DeviceIdType.MESH
HIGH = lax.Precision.HIGHEST


def dot(a, b):
    return lax.dot_general(
        a, b, (((1,), (0,)), ((), ())), precision=HIGH, preferred_element_type=jnp.float32
    )


class Reducer:
    def __init__(self, place, src, first, second, full, sems):
        self.place, self.src, self.first, self.second, self.full = place, src, first, second, full
        self.s1, self.r1, self.s2, self.r2, self.s3, self.r3 = sems
        self.chunk = src.shape[0] // GROUP

    def rows(self, t):
        return pl.ds(pl.multiple_of(t * self.chunk, 8), self.chunk)

    def copy1(self, j):
        t = self.place.member(j)
        return pltpu.make_async_remote_copy(
            self.src.at[self.rows(t)], self.first.at[j - 1], self.s1.at[j - 1], self.r1.at[j - 1],
            device_id=self.place.group_id(t), device_id_type=MESH)

    def copy2(self, j, slot, to):
        return pltpu.make_async_remote_copy(
            self.second.at[slot], self.second.at[slot], self.s2.at[j - 1], self.r2.at[slot],
            device_id=self.place.slab_id(to), device_id_type=MESH)

    def copy3(self, j, owner):
        t = self.place.member(j)
        return pltpu.make_async_remote_copy(
            self.full.at[self.rows(owner)], self.full.at[self.rows(owner)],
            self.s3.at[j - 1], self.r3.at[j - 1],
            device_id=self.place.group_id(t), device_id_type=MESH)

    def start1(self):
        for j in range(1, GROUP):
            self.copy1(j).start()

    def start2(self):
        place = self.place
        total = self.src[self.rows(place.g)]
        for j in range(1, GROUP):
            self.copy1(j).wait_recv()
            total = total + self.first[j - 1]
        self.second[place.z] = total
        for j in range(1, place.slabs):
            self.copy2(j, place.z, lax.rem(place.z + j, place.slabs)).start()

    def start3(self):
        place = self.place
        for j in range(1, place.slabs):
            other = lax.rem(place.z + j, place.slabs)
            self.copy2(j, other, other).wait_recv()
        total = self.second[0]
        for i in range(1, place.slabs):
            total = total + self.second[i]
        self.full[self.rows(place.g)] = total
        for j in range(1, GROUP):
            self.copy3(j, place.g).start()

    def finish(self):
        place = self.place
        for j in range(1, GROUP):
            self.copy3(j, place.member(GROUP - j)).wait_recv()
        for j in range(1, GROUP):
            self.copy1(j).wait_send()
            self.copy3(j, place.g).wait_send()
        for j in range(1, place.slabs):
            self.copy2(j, place.z, lax.rem(place.z + j, place.slabs)).wait_send()


class Place:
    def __init__(self, slabs):
        self.s = lax.axis_index("shift")
        self.p = lax.axis_index("space")
        self.b = lax.rem(self.p, 2)
        self.z = self.p // 2
        self.g = self.s * 2 + self.b
        self.slabs = slabs

    def member(self, j):
        return lax.rem(self.g + j, GROUP)

    def group_id(self, t):
        return (t // 2, self.z * 2 + lax.rem(t, 2))

    def slab_id(self, z):
        return (self.s, z * 2 + self.b)


def split(x):
    hi = x.astype(jnp.bfloat16)
    return hi, (x - hi.astype(jnp.float32)).astype(jnp.bfloat16)


def raw(a, b, dims):
    return lax.dot_general(a, b, (dims, ((), ())), preferred_element_type=jnp.float32)


def dot3(a_hi, a_lo, b_hi, b_lo, dims):
    rows = a_hi.shape[0]
    both = raw(jnp.concatenate([a_hi, a_lo], axis=0), b_hi, dims)
    return both[:rows] + (both[rows:] + raw(a_hi, b_lo, dims))


TRANSPOSED = ((1,), (1,))
PLAIN = ((1,), (0,))


def kernel(slabs, cell_weight, labels_hbm, cond_hbm, capa_hbm, shift_hbm, q_hbm,
           out_ref, coef_ref, fac_ref,
           lab, kap, cap, face, dg, rc, rem, sol, dirs, wt, qn, qs, qh, ql, wh, wl,
           gsrc, gfirst, gsecond, gfull, psrc, pfirst, psecond, pfull,
           cross, cond_ref, capa_ref, shift_ref,
           lab_s, lab_r, in_s, in_r, out_s, out_r, halo_s, halo_r, loc, qsem, osem, gsem, psem):
    place = Place(slabs)
    s, b, z, g = place.s, place.b, place.z, place.g
    f32 = jnp.float32
    basis, slab_x, quarter, depth = q_hbm.shape
    new = wt.shape[2]
    cells = slab_x * quarter
    rows_y = lab.shape[1]
    old = basis - new

    def load(k, first, count, i):
        return pltpu.make_async_copy(
            qn.at[pl.ds(first, count), k // quarter, k % quarter, :],
            qs.at[k // quarter, k % quarter, pl.ds(first, count), :], qsem.at[i, k])

    fetch = [pltpu.make_async_copy(q_hbm.at[pl.ds(first, count)], qn.at[pl.ds(first, count)], loc.at[6 + i])
             for i, (first, count) in enumerate([(old, new), (0, old)])]
    fetch[0].start()
    own_lab = pltpu.make_async_copy(labels_hbm, lab.at[pl.ds(1 + 2 * b, 2)], loc.at[2])
    own_lab.start()
    tables = [pltpu.make_async_copy(src, dst, loc.at[3 + i]) for i, (src, dst) in enumerate(
        [(cond_hbm, cond_ref), (capa_hbm, capa_ref), (shift_hbm, shift_ref)])]
    for copy in tables:
        copy.start()
    fetch[1].start()
    fetch[0].wait()
    for k in range(cells):
        load(k, old, new, 0).start()

    barrier = pltpu.get_barrier_semaphore()
    for j in range(1, GROUP):
        pl.semaphore_signal(barrier, inc=1, device_id=place.group_id(place.member(j)), device_id_type=MESH)
    for j in range(1, slabs):
        pl.semaphore_signal(barrier, inc=1, device_id=place.slab_id(lax.rem(z + j, slabs)), device_id_type=MESH)
    for n in range(SWEEPS - 1):
        for i in range(1, 5):
            dirs[n, i, 0] = jnp.zeros((COLS, depth), f32)
            dirs[n, i, rows_y + 1] = jnp.zeros((COLS, depth), f32)
    pl.semaphore_wait(barrier, GROUP - 1 + slabs - 1)

    pair = lax.rem(b + 1, 2)

    def lab_pair(owner):
        return pltpu.make_async_remote_copy(
            labels_hbm, lab.at[pl.ds(1 + 2 * owner, 2)], lab_s.at[0], lab_r.at[0],
            device_id=(s, z * 2 + pair), device_id_type=MESH)

    def edge(from_plane, to_plane, k, to):
        return pltpu.make_async_remote_copy(
            lab.at[from_plane], lab.at[to_plane], lab_s.at[k], lab_r.at[k],
            device_id=place.slab_id(to), device_id_type=MESH)

    def slot(field, t):
        return field.at[pl.ds(lax.rem(t, 2) * 2, 2), pl.ds((t // 2) * quarter, quarter)]

    def copy_in(j, to, owner):
        return pltpu.make_async_remote_copy(
            qs.at[:, :, pl.ds(pl.multiple_of(old + to * COLS, COLS), COLS), :], slot(rem, owner),
            in_s.at[j - 1], in_r.at[j - 1], device_id=place.group_id(to), device_id_type=MESH)

    lab_pair(b).start()
    for k in range(cells):
        load(k, old, new, 0).wait()
    for j in range(1, GROUP):
        copy_in(j, place.member(j), g).start()
    mine = pltpu.make_async_copy(
        qs.at[:, :, pl.ds(pl.multiple_of(old + g * COLS, COLS), COLS), :], slot(rem, g), loc.at[0])
    mine.start()
    fetch[1].wait()
    for k in range(cells):
        load(k, 0, old, 1).start()
    own_lab.wait()
    lab_pair(pair).wait_recv()

    @pl.when(z > 0)
    def _():
        edge(1, 5, 1, z - 1).start()

    @pl.when(z < slabs - 1)
    def _():
        edge(4, 0, 2, z + 1).start()

    for end, there in ((0, z == 0), (5, z == slabs - 1)):
        @pl.when(there)
        def _():
            lab[end] = jnp.full((rows_y, depth), -1, jnp.int32)
            for n in range(SWEEPS - 1):
                dirs[n, end] = jnp.zeros((rows_y + 2, COLS, depth), f32)

    for k in range(cells):
        load(k, 0, old, 1).wait()
    gsrc[...] = jnp.zeros_like(gsrc)
    cross[...] = jnp.zeros_like(cross)

    @pl.loop(0, cells)
    def _(k):
        hi, lo = split(qs[k // quarter, lax.rem(k, quarter)])
        qh[k] = hi
        ql[k] = lo
        gsrc[...] += raw(hi, hi, TRANSPOSED)
        cross[...] += raw(hi, lo, TRANSPOSED)

    gsrc[...] += cross[...] + cross[...].T

    @pl.when(z > 0)
    def _():
        edge(4, 0, 2, z - 1).wait_recv()

    @pl.when(z < slabs - 1)
    def _():
        edge(1, 5, 1, z + 1).wait_recv()

    for copy in tables:
        copy.wait()

    @pl.loop(0, 6)
    def _(i):
        value = lab[i]
        k_acc = jnp.zeros((rows_y, depth), f32)
        for m in range(cond_ref.shape[0]):
            k_acc = jnp.where(value == m, cond_ref[m], k_acc)
        kap[i] = k_acc

    shift = shift_ref[g]
    row = lax.broadcasted_iota(jnp.int32, (rows_y, depth), 0)
    lane = lax.broadcasted_iota(jnp.int32, (rows_y, depth), 1)

    @pl.loop(0, 4)
    def _(i):
        value = lab[i + 1]
        c_acc = jnp.zeros((rows_y, depth), f32)
        for m in range(capa_ref.shape[0]):
            c_acc = jnp.where(value == m, capa_ref[m], c_acc)
        cap[i] = c_acc
        me = kap[i + 1]
        zero = jnp.zeros_like(me)
        west = 0.5 * (me + kap[i])
        east = 0.5 * (me + kap[i + 2])
        south = 0.5 * (me + jnp.where(row == 0, zero, pltpu.roll(me, 1, 0)))
        north = 0.5 * (me + jnp.where(row == rows_y - 1, zero, pltpu.roll(me, rows_y - 1, 0)))
        below = 0.5 * (me + jnp.where(lane == 0, zero, pltpu.roll(me, 1, 1)))
        above = 0.5 * (me + jnp.where(lane == depth - 1, zero, pltpu.roll(me, depth - 1, 1)))
        diag = ((west + east) + (south + north)) + (below + above) + shift * c_acc
        dg[i] = diag
        rc[i] = 1.0 / diag
        face[0, i] = west
        face[1, i] = east
        face[2, i] = south
        face[3, i] = north
        face[4, i] = jnp.where(lane == 0, zero, below)
        face[5, i] = jnp.where(lane == depth - 1, zero, above)

    greduce = Reducer(place, gsrc, gfirst, gsecond, gfull, [gsem.at[i] for i in range(6)])

    mine.wait()
    for j in range(1, GROUP):
        copy_in(j, place.member(j), place.member(GROUP - j)).wait_recv()
    greduce.start1()

    center = 0.5 * (UPPER_BOUND + LOWER_BOUND)
    spread = 0.5 * (UPPER_BOUND - LOWER_BOUND)
    ratio = center / spread

    def begin(i):
        @pl.loop(0, rows_y // 8)
        def _(t):
            tile = pl.ds(pl.multiple_of(t * 8, 8), 8)
            c_t, rc_t = cap[i, tile], rc[i, tile]
            for u in range(8):
                y = t * 8 + u
                r = rem[i, y] * c_t[u:u + 1]
                d = (rc_t[u:u + 1] * r) / center
                rem[i, y] = r
                sol[i, y] = d
                dirs[0, i + 1, y + 1] = d

    def sweep(n, i, keep, step):
        @pl.loop(0, rows_y // 8)
        def _(t):
            tile = pl.ds(pl.multiple_of(t * 8, 8), 8)
            f = [face[k, i, tile] for k in range(6)]
            dg_t, rc_t = dg[i, tile], rc[i, tile]
            for u in range(8):
                y = t * 8 + u
                w_, e_, s_, n_, b_, a_ = [v[u:u + 1] for v in f]
                d = dirs[n, i + 1, y + 1]
                near = w_ * dirs[n, i, y + 1] + e_ * dirs[n, i + 2, y + 1]
                near = near + s_ * dirs[n, i + 1, y] + n_ * dirs[n, i + 1, y + 2]
                near = near + b_ * pltpu.roll(d, 1, 1) + a_ * pltpu.roll(d, depth - 1, 1)
                r = rem[i, y] - (dg_t[u:u + 1] * d - near)
                nd = keep * d + step * (rc_t[u:u + 1] * r)
                sol[i, y] = sol[i, y] + nd
                if n + 1 < SWEEPS - 1:
                    rem[i, y] = r
                    dirs[n + 1, i + 1, y + 1] = nd

    def halo(n, src, dst, k, to):
        return pltpu.make_async_remote_copy(
            dirs.at[n, src, pl.ds(1, rows_y)], dirs.at[n, dst, pl.ds(1, rows_y)],
            halo_s.at[n, k], halo_r.at[n, k], device_id=place.slab_id(to), device_id_type=MESH)

    def send_halo(n):
        @pl.when(z > 0)
        def _():
            halo(n, 1, 5, 0, z - 1).start()

        @pl.when(z < slabs - 1)
        def _():
            halo(n, 4, 0, 1, z + 1).start()

    begin(0)
    begin(3)
    send_halo(0)
    begin(1)
    begin(2)
    weight_old = 1.0 / ratio
    for n in range(SWEEPS - 1):
        weight = 1.0 / (2.0 * ratio - weight_old)
        keep, step = weight * weight_old, 2.0 * weight / spread
        weight_old = weight
        sweep(n, 1, keep, step)
        sweep(n, 2, keep, step)
        if n == 0:
            greduce.start2()
        if n == 1:
            greduce.start3()
        if n == 2:
            greduce.finish()

        @pl.when(z > 0)
        def _():
            halo(n, 4, 0, 1, z - 1).wait_recv()

        @pl.when(z < slabs - 1)
        def _():
            halo(n, 1, 5, 0, z + 1).wait_recv()

        sweep(n, 0, keep, step)
        sweep(n, 3, keep, step)
        if n + 1 < SWEEPS - 1:
            send_halo(n + 1)

    def copy_out(j, to, owner):
        return pltpu.make_async_remote_copy(
            slot(sol, to), wt.at[:, :, pl.ds(pl.multiple_of(owner * COLS, COLS), COLS), :],
            out_s.at[j - 1], out_r.at[j - 1], device_id=place.group_id(to), device_id_type=MESH)

    for j in range(1, GROUP):
        copy_out(j, place.member(j), g).start()
    back = pltpu.make_async_copy(
        slot(sol, g), wt.at[:, :, pl.ds(pl.multiple_of(g * COLS, COLS), COLS), :], loc.at[1])
    back.start()

    lab_pair(b).wait_send()

    @pl.when(z > 0)
    def _():
        edge(1, 5, 1, z - 1).wait_send()
        for n in range(SWEEPS - 1):
            halo(n, 1, 5, 0, z - 1).wait_send()

    @pl.when(z < slabs - 1)
    def _():
        edge(4, 0, 2, z + 1).wait_send()
        for n in range(SWEEPS - 1):
            halo(n, 4, 0, 1, z + 1).wait_send()

    for j in range(1, GROUP):
        copy_in(j, place.member(j), g).wait_send()
    psrc[...] = jnp.zeros_like(psrc)
    back.wait()
    for j in range(1, GROUP):
        copy_out(j, place.member(j), place.member(GROUP - j)).wait_recv()

    @pl.loop(0, cells // 4)
    def _(k4):
        total = psrc[:, :basis]
        same = psrc[:, basis:basis + new]
        for i in range(4):
            k = k4 * 4 + i
            w = wt[k // quarter, lax.rem(k, quarter)]
            hi, lo = split(w)
            total = total + dot3(hi, lo, qh[k], ql[k], TRANSPOSED)
            same = same + lax.dot_general(
                w, w, (TRANSPOSED, ((), ())), precision=HIGH, preferred_element_type=f32)
        psrc[:, :basis] = total
        psrc[:, basis:basis + new] = same

    preduce = Reducer(place, psrc, pfirst, psecond, pfull, [psem.at[i] for i in range(6)])
    preduce.start1()
    preduce.start2()
    preduce.start3()
    for j in range(1, GROUP):
        copy_out(j, place.member(j), g).wait_send()
    preduce.finish()

    proj = pfull[:, :basis] * cell_weight
    own_gram = pfull[:, basis:basis + new] * cell_weight
    basis_gram = gfull[...] * cell_weight
    coef = proj + (proj - dot(proj, basis_gram))
    coef_ref[...] = coef
    coef_hi, coef_lo = split(coef)

    half = dot(coef, basis_gram) * 0.5 - proj
    turn = lax.dot_general(coef, half, (TRANSPOSED, ((), ())), precision=HIGH, preferred_element_type=f32)
    gram = own_gram + (turn + turn.T)

    r64 = lax.broadcasted_iota(jnp.int32, (new, new), 0)
    c64 = lax.broadcasted_iota(jnp.int32, (new, new), 1)
    eye = jnp.where(r64 == c64, 1.0, 0.0).astype(f32)
    work = jnp.concatenate([gram, eye], axis=1)
    per = new // cells
    for k in range(cells):
        for j in range(k * per, min((k + 1) * per, new - 1)):
            lo = (j // 8) * 8
            live = work[lo:]
            pivot_row = work[j:j + 1]
            scaled = pivot_row / pivot_row[:, j:j + 1]
            col = live[:, j:j + 1]
            below_pivot = lax.broadcasted_iota(jnp.int32, (new - lo, 1), 0) > (j - lo)
            live = live - jnp.where(below_pivot, col, 0.0) * scaled
            work = jnp.concatenate([work[:lo], live], axis=0) if lo else live
        w2 = wt[k // quarter, k % quarter] - dot3(coef_hi, coef_lo, qh[k], ql[k], PLAIN)
        wh[k], wl[k] = split(w2)
    diag = jnp.sum(jnp.where(r64 == c64, work[:, :new], 0.0), axis=1, keepdims=True)
    work = work / jnp.sqrt(diag)
    upper = jnp.where(c64 >= r64, work[:, :new], 0.0)
    fac_ref[...] = lax.dot_general(
        upper, eye, (((0,), (0,)), ((), ())), precision=HIGH, preferred_element_type=f32)
    inv_hi, inv_lo = split(work[:, new:])

    def result(k):
        return pltpu.make_async_copy(
            wt.at[k // quarter, k % quarter], out_ref.at[:, k // quarter, k % quarter, :], osem.at[k])

    for k in range(cells):
        wt[k // quarter, k % quarter] = dot3(inv_hi, inv_lo, wh[k], wl[k], PLAIN)
        result(k).start()
    for k in range(cells):
        result(k).wait()


def local(slabs, labels, conductance, capacity_table, shift_values, prior_basis):
    basis, slab_x, quarter, depth = prior_basis.shape
    shifts = shift_values.shape[0]
    new = shifts * COLS
    rows_y = labels.shape[1]
    cells = slab_x * quarter
    count = cells * depth * lax.axis_size("shift") * lax.axis_size("space")
    f32 = jnp.float32

    def reducer(rows, lanes):
        c = rows // GROUP
        return [pltpu.VMEM((rows, lanes), f32), pltpu.VMEM((GROUP - 1, c, lanes), f32),
                pltpu.VMEM((slabs, c, lanes), f32), pltpu.VMEM((rows, lanes), f32)]

    dma = pltpu.SemaphoreType.DMA
    width = max(GROUP, slabs)
    vmem = pl.BlockSpec(memory_space=pltpu.VMEM)
    block, coef, factor = pl.pallas_call(
        functools.partial(kernel, slabs, 1.0 / count),
        out_shape=[
            jax.ShapeDtypeStruct((new, slab_x, quarter, depth), f32),
            jax.ShapeDtypeStruct((new, basis), f32),
            jax.ShapeDtypeStruct((new, new), f32),
        ],
        in_specs=[pl.BlockSpec(memory_space=pltpu.HBM)] * 5,
        out_specs=[vmem] * 3,
        scratch_shapes=[
            pltpu.VMEM((6, rows_y, depth), jnp.int32),
            pltpu.VMEM((6, rows_y, depth), f32),
            pltpu.VMEM((4, rows_y, depth), f32),
            pltpu.VMEM((6, 4, rows_y, depth), f32),
            pltpu.VMEM((4, rows_y, depth), f32),
            pltpu.VMEM((4, rows_y, depth), f32),
            pltpu.VMEM((4, rows_y, COLS, depth), f32),
            pltpu.VMEM((4, rows_y, COLS, depth), f32),
            pltpu.VMEM((SWEEPS - 1, 6, rows_y + 2, COLS, depth), f32),
            pltpu.VMEM((slab_x, quarter, new, depth), f32),
            pltpu.VMEM((basis, slab_x, quarter, depth), f32),
            pltpu.VMEM((slab_x, quarter, basis, depth), f32),
            pltpu.VMEM((cells, basis, depth), jnp.bfloat16),
            pltpu.VMEM((cells, basis, depth), jnp.bfloat16),
            pltpu.VMEM((cells, new, depth), jnp.bfloat16),
            pltpu.VMEM((cells, new, depth), jnp.bfloat16),
            *reducer(basis, basis),
            *reducer(new, basis + 128),
            pltpu.VMEM((basis, basis), f32),
            pltpu.SMEM(conductance.shape, f32),
            pltpu.SMEM(capacity_table.shape, f32),
            pltpu.SMEM(shift_values.shape, f32),
            dma((3,)), dma((3,)), dma((GROUP - 1,)), dma((GROUP - 1,)),
            dma((GROUP - 1,)), dma((GROUP - 1,)), dma((SWEEPS - 1, 2)), dma((SWEEPS - 1, 2)),
            dma((8,)), dma((2, cells)), dma((cells,)),
            dma((6, width)), dma((6, width)),
        ],
        compiler_params=pltpu.CompilerParams(
            collective_id=0, has_side_effects=True, vmem_limit_bytes=48 * 1024 * 1024),
    )(labels, conductance, capacity_table, shift_values, prior_basis)
    return block.reshape(shifts, COLS, slab_x, quarter, depth), coef, factor


def solution(mesh):
    in_specs = (P("space", None, None), P(), P(), P(), P(None, "space", "shift", None))
    out_specs = (P(None, None, "space", "shift", None), P(), P())
    slabs = mesh.shape["space"] // 2
    return jax.shard_map(
        functools.partial(local, slabs), mesh=mesh, in_specs=in_specs, out_specs=out_specs, check_vma=False)
```

```python
import functools

import jax
import jax.numpy as jnp
from jax import lax
from jax.experimental import pallas as pl
from jax.experimental.pallas import tpu as pltpu
from jax.sharding import PartitionSpec as P

COLS = 8
SWEEPS = 4
GROUP = 8
LOWER_BOUND = 0.1
UPPER_BOUND = 2.0
MESH = pl.DeviceIdType.MESH
HIGH = lax.Precision.HIGHEST


def dot(a, b):
    return lax.dot_general(
        a, b, (((1,), (0,)), ((), ())), precision=HIGH, preferred_element_type=jnp.float32
    )


class Reducer:
    def __init__(self, place, src, first, second, full, sems):
        self.place, self.src, self.first, self.second, self.full = place, src, first, second, full
        self.s1, self.r1, self.s2, self.r2, self.s3, self.r3 = sems
        self.chunk = src.shape[0] // GROUP

    def rows(self, t):
        return pl.ds(pl.multiple_of(t * self.chunk, 8), self.chunk)

    def copy1(self, j):
        t = self.place.member(j)
        return pltpu.make_async_remote_copy(
            self.src.at[self.rows(t)], self.first.at[j - 1], self.s1.at[j - 1], self.r1.at[j - 1],
            device_id=self.place.group_id(t), device_id_type=MESH)

    def copy2(self, j, slot, to):
        return pltpu.make_async_remote_copy(
            self.second.at[slot], self.second.at[slot], self.s2.at[j - 1], self.r2.at[slot],
            device_id=self.place.slab_id(to), device_id_type=MESH)

    def copy3(self, j, owner):
        t = self.place.member(j)
        return pltpu.make_async_remote_copy(
            self.full.at[self.rows(owner)], self.full.at[self.rows(owner)],
            self.s3.at[j - 1], self.r3.at[j - 1],
            device_id=self.place.group_id(t), device_id_type=MESH)

    def start1(self):
        for j in range(1, GROUP):
            self.copy1(j).start()

    def start2(self):
        place = self.place
        total = self.src[self.rows(place.g)]
        for j in range(1, GROUP):
            self.copy1(j).wait_recv()
            total = total + self.first[j - 1]
        self.second[place.z] = total
        for j in range(1, place.slabs):
            self.copy2(j, place.z, lax.rem(place.z + j, place.slabs)).start()

    def start3(self):
        place = self.place
        for j in range(1, place.slabs):
            other = lax.rem(place.z + j, place.slabs)
            self.copy2(j, other, other).wait_recv()
        total = self.second[0]
        for i in range(1, place.slabs):
            total = total + self.second[i]
        self.full[self.rows(place.g)] = total
        for j in range(1, GROUP):
            self.copy3(j, place.g).start()

    def finish(self):
        place = self.place
        for j in range(1, GROUP):
            self.copy3(j, place.member(GROUP - j)).wait_recv()
        for j in range(1, GROUP):
            self.copy1(j).wait_send()
            self.copy3(j, place.g).wait_send()
        for j in range(1, place.slabs):
            self.copy2(j, place.z, lax.rem(place.z + j, place.slabs)).wait_send()


class Place:
    def __init__(self, slabs):
        self.s = lax.axis_index("shift")
        self.p = lax.axis_index("space")
        self.b = lax.rem(self.p, 2)
        self.z = self.p // 2
        self.g = self.s * 2 + self.b
        self.slabs = slabs

    def member(self, j):
        return lax.rem(self.g + j, GROUP)

    def group_id(self, t):
        return (t // 2, self.z * 2 + lax.rem(t, 2))

    def slab_id(self, z):
        return (self.s, z * 2 + self.b)


def split(x):
    hi = x.astype(jnp.bfloat16)
    return hi, (x - hi.astype(jnp.float32)).astype(jnp.bfloat16)


def raw(a, b, dims):
    return lax.dot_general(a, b, (dims, ((), ())), preferred_element_type=jnp.float32)


def dot3(a_hi, a_lo, b_hi, b_lo, dims):
    rows = a_hi.shape[0]
    both = raw(jnp.concatenate([a_hi, a_lo], axis=0), b_hi, dims)
    return both[:rows] + (both[rows:] + raw(a_hi, b_lo, dims))


TRANSPOSED = ((1,), (1,))
PLAIN = ((1,), (0,))


def kernel(slabs, cell_weight, labels_hbm, cond_hbm, capa_hbm, shift_hbm, q_hbm,
           out_ref, coef_ref, fac_ref,
           lab, kap, cap, face, dg, rc, rem, sol, dirs, wt, qn, qs, qh, ql, wh, wl,
           gsrc, gfirst, gsecond, gfull, psrc, pfirst, psecond, pfull,
           cross, cond_ref, capa_ref, shift_ref,
           lab_s, lab_r, in_s, in_r, out_s, out_r, halo_s, halo_r, loc, qsem, osem, gsem, psem):
    place = Place(slabs)
    s, b, z, g = place.s, place.b, place.z, place.g
    f32 = jnp.float32
    basis, slab_x, quarter, depth = q_hbm.shape
    new = wt.shape[2]
    cells = slab_x * quarter
    rows_y = lab.shape[1]
    old = basis - new

    def load(k, first, count, i):
        return pltpu.make_async_copy(
            qn.at[pl.ds(first, count), k // quarter, k % quarter, :],
            qs.at[k // quarter, k % quarter, pl.ds(first, count), :], qsem.at[i, k])

    fetch = [pltpu.make_async_copy(q_hbm.at[pl.ds(first, count)], qn.at[pl.ds(first, count)], loc.at[6 + i])
             for i, (first, count) in enumerate([(old, new), (0, old)])]
    fetch[0].start()
    own_lab = pltpu.make_async_copy(labels_hbm, lab.at[pl.ds(1 + 2 * b, 2)], loc.at[2])
    own_lab.start()
    tables = [pltpu.make_async_copy(src, dst, loc.at[3 + i]) for i, (src, dst) in enumerate(
        [(cond_hbm, cond_ref), (capa_hbm, capa_ref), (shift_hbm, shift_ref)])]
    for copy in tables:
        copy.start()
    fetch[1].start()
    fetch[0].wait()
    for k in range(cells):
        load(k, old, new, 0).start()

    barrier = pltpu.get_barrier_semaphore()
    for j in range(1, GROUP):
        pl.semaphore_signal(barrier, inc=1, device_id=place.group_id(place.member(j)), device_id_type=MESH)
    for j in range(1, slabs):
        pl.semaphore_signal(barrier, inc=1, device_id=place.slab_id(lax.rem(z + j, slabs)), device_id_type=MESH)
    for n in range(SWEEPS - 1):
        for i in range(1, 5):
            dirs[n, i, 0] = jnp.zeros((COLS, depth), f32)
            dirs[n, i, rows_y + 1] = jnp.zeros((COLS, depth), f32)
    pl.semaphore_wait(barrier, GROUP - 1 + slabs - 1)

    pair = lax.rem(b + 1, 2)

    def lab_pair(owner):
        return pltpu.make_async_remote_copy(
            labels_hbm, lab.at[pl.ds(1 + 2 * owner, 2)], lab_s.at[0], lab_r.at[0],
            device_id=(s, z * 2 + pair), device_id_type=MESH)

    def edge(from_plane, to_plane, k, to):
        return pltpu.make_async_remote_copy(
            lab.at[from_plane], lab.at[to_plane], lab_s.at[k], lab_r.at[k],
            device_id=place.slab_id(to), device_id_type=MESH)

    def plane_of(member_b, part):
        return member_b if part == 0 else 1 - member_b

    def column(t):
        return pl.ds(pl.multiple_of(t * COLS, COLS), COLS)

    def slot(field, t, part):
        tb = lax.rem(t, 2)
        return field.at[2 * tb + plane_of(tb, part), pl.ds((t // 2) * quarter, quarter)]

    def tail(t, part):
        return qs.at[plane_of(b, part), :, pl.ds(pl.multiple_of(old + t * COLS, COLS), COLS), :]

    def copy_in(j, to, owner, part):
        return pltpu.make_async_remote_copy(
            tail(to, part), slot(rem, owner, part), in_s.at[part, j - 1], in_r.at[part, j - 1],
            device_id=place.group_id(to), device_id_type=MESH)

    lab_pair(b).start()
    for k in range(cells):
        load(k, old, new, 0).wait()
    for part in (0, 1):
        for j in range(1, GROUP):
            copy_in(j, place.member(j), g, part).start()
    mine = [pltpu.make_async_copy(tail(g, part), slot(rem, g, part), loc.at[8 * part]) for part in (0, 1)]
    for copy in mine:
        copy.start()
    fetch[1].wait()
    for k in range(cells):
        load(k, 0, old, 1).start()
    own_lab.wait()
    lab_pair(pair).wait_recv()

    @pl.when(z > 0)
    def _():
        edge(1, 5, 1, z - 1).start()

    @pl.when(z < slabs - 1)
    def _():
        edge(4, 0, 2, z + 1).start()

    for end, there in ((0, z == 0), (5, z == slabs - 1)):
        @pl.when(there)
        def _():
            lab[end] = jnp.full((rows_y, depth), -1, jnp.int32)
            for n in range(SWEEPS - 1):
                dirs[n, end] = jnp.zeros((rows_y + 2, COLS, depth), f32)

    for k in range(cells):
        load(k, 0, old, 1).wait()
    gsrc[...] = jnp.zeros_like(gsrc)
    cross[...] = jnp.zeros_like(cross)

    @pl.loop(0, cells)
    def _(k):
        hi, lo = split(qs[k // quarter, lax.rem(k, quarter)])
        qh[k] = hi
        ql[k] = lo
        gsrc[...] += raw(hi, hi, TRANSPOSED)
        cross[...] += raw(hi, lo, TRANSPOSED)

    gsrc[...] += cross[...] + cross[...].T

    @pl.when(z > 0)
    def _():
        edge(4, 0, 2, z - 1).wait_recv()

    @pl.when(z < slabs - 1)
    def _():
        edge(1, 5, 1, z + 1).wait_recv()

    for copy in tables:
        copy.wait()

    @pl.loop(0, 6)
    def _(i):
        value = lab[i]
        k_acc = jnp.zeros((rows_y, depth), f32)
        for m in range(cond_ref.shape[0]):
            k_acc = jnp.where(value == m, cond_ref[m], k_acc)
        kap[i] = k_acc

    shift = shift_ref[g]
    row = lax.broadcasted_iota(jnp.int32, (rows_y, depth), 0)
    lane = lax.broadcasted_iota(jnp.int32, (rows_y, depth), 1)

    @pl.loop(0, 4)
    def _(i):
        value = lab[i + 1]
        c_acc = jnp.zeros((rows_y, depth), f32)
        for m in range(capa_ref.shape[0]):
            c_acc = jnp.where(value == m, capa_ref[m], c_acc)
        cap[i] = c_acc
        me = kap[i + 1]
        zero = jnp.zeros_like(me)
        west = 0.5 * (me + kap[i])
        east = 0.5 * (me + kap[i + 2])
        south = 0.5 * (me + jnp.where(row == 0, zero, pltpu.roll(me, 1, 0)))
        north = 0.5 * (me + jnp.where(row == rows_y - 1, zero, pltpu.roll(me, rows_y - 1, 0)))
        below = 0.5 * (me + jnp.where(lane == 0, zero, pltpu.roll(me, 1, 1)))
        above = 0.5 * (me + jnp.where(lane == depth - 1, zero, pltpu.roll(me, depth - 1, 1)))
        diag = ((west + east) + (south + north)) + (below + above) + shift * c_acc
        dg[i] = diag
        rc[i] = 1.0 / diag
        face[0, i] = west
        face[1, i] = east
        face[2, i] = south
        face[3, i] = north
        face[4, i] = jnp.where(lane == 0, zero, below)
        face[5, i] = jnp.where(lane == depth - 1, zero, above)

    greduce = Reducer(place, gsrc, gfirst, gsecond, gfull, [gsem.at[i] for i in range(6)])

    def arrived(part):
        mine[part].wait()
        for j in range(1, GROUP):
            copy_in(j, place.member(j), place.member(GROUP - j), part).wait_recv()

    center = 0.5 * (UPPER_BOUND + LOWER_BOUND)
    spread = 0.5 * (UPPER_BOUND - LOWER_BOUND)
    ratio = center / spread

    def begin(i):
        @pl.loop(0, rows_y // 8)
        def _(t):
            tile = pl.ds(pl.multiple_of(t * 8, 8), 8)
            c_t, rc_t = cap[i, tile], rc[i, tile]
            for u in range(8):
                y = t * 8 + u
                r = rem[i, y] * c_t[u:u + 1]
                d = (rc_t[u:u + 1] * r) / center
                rem[i, y] = r
                sol[i, y] = d
                dirs[0, i + 1, y + 1] = d

    def sweep(n, i, keep, step):
        @pl.loop(0, rows_y // 8)
        def _(t):
            tile = pl.ds(pl.multiple_of(t * 8, 8), 8)
            f = [face[k, i, tile] for k in range(6)]
            dg_t, rc_t = dg[i, tile], rc[i, tile]
            for u in range(8):
                y = t * 8 + u
                w_, e_, s_, n_, b_, a_ = [v[u:u + 1] for v in f]
                d = dirs[n, i + 1, y + 1]
                near = w_ * dirs[n, i, y + 1] + e_ * dirs[n, i + 2, y + 1]
                near = near + s_ * dirs[n, i + 1, y] + n_ * dirs[n, i + 1, y + 2]
                near = near + b_ * pltpu.roll(d, 1, 1) + a_ * pltpu.roll(d, depth - 1, 1)
                r = rem[i, y] - (dg_t[u:u + 1] * d - near)
                nd = keep * d + step * (rc_t[u:u + 1] * r)
                sol[i, y] = sol[i, y] + nd
                if n + 1 < SWEEPS - 1:
                    rem[i, y] = r
                    dirs[n + 1, i + 1, y + 1] = nd

    def halo(n, src, dst, k, to):
        return pltpu.make_async_remote_copy(
            dirs.at[n, src, pl.ds(1, rows_y)], dirs.at[n, dst, pl.ds(1, rows_y)],
            halo_s.at[n, k], halo_r.at[n, k], device_id=place.slab_id(to), device_id_type=MESH)

    def send_halo(n):
        @pl.when(z > 0)
        def _():
            halo(n, 1, 5, 0, z - 1).start()

        @pl.when(z < slabs - 1)
        def _():
            halo(n, 4, 0, 1, z + 1).start()

    arrived(0)
    begin(0)
    begin(3)
    send_halo(0)
    arrived(1)
    greduce.start1()
    begin(1)
    begin(2)
    def copy_out(j, to, owner, part, reader_b):
        return pltpu.make_async_remote_copy(
            slot(sol, to, part), wt.at[plane_of(reader_b, part), :, column(owner), :],
            out_s.at[part, j - 1], out_r.at[part, j - 1],
            device_id=place.group_id(to), device_id_type=MESH)

    back = [pltpu.make_async_copy(
        slot(sol, g, part), wt.at[plane_of(b, part), :, column(g), :], loc.at[1 + 8 * part]) for part in (0, 1)]

    def send_out(part):
        for j in range(1, GROUP):
            to = place.member(j)
            copy_out(j, to, g, part, lax.rem(to, 2)).start()
        back[part].start()

    weight_old = 1.0 / ratio
    for n in range(SWEEPS - 1):
        weight = 1.0 / (2.0 * ratio - weight_old)
        keep, step = weight * weight_old, 2.0 * weight / spread
        weight_old = weight
        sweep(n, 1, keep, step)
        sweep(n, 2, keep, step)
        if n == SWEEPS - 2:
            send_out(1)
        if n == 0:
            greduce.start2()
        if n == 1:
            greduce.start3()
        if n == 2:
            greduce.finish()

        @pl.when(z > 0)
        def _():
            halo(n, 4, 0, 1, z - 1).wait_recv()

        @pl.when(z < slabs - 1)
        def _():
            halo(n, 1, 5, 0, z + 1).wait_recv()

        sweep(n, 0, keep, step)
        sweep(n, 3, keep, step)
        if n + 1 < SWEEPS - 1:
            send_halo(n + 1)

    send_out(0)

    lab_pair(b).wait_send()

    @pl.when(z > 0)
    def _():
        edge(1, 5, 1, z - 1).wait_send()
        for n in range(SWEEPS - 1):
            halo(n, 1, 5, 0, z - 1).wait_send()

    @pl.when(z < slabs - 1)
    def _():
        edge(4, 0, 2, z + 1).wait_send()
        for n in range(SWEEPS - 1):
            halo(n, 4, 0, 1, z + 1).wait_send()

    for part in (0, 1):
        for j in range(1, GROUP):
            copy_in(j, place.member(j), g, part).wait_send()
    psrc[...] = jnp.zeros_like(psrc)
    for part in (1, 0):
        back[part].wait()
        for j in range(1, GROUP):
            copy_out(j, place.member(j), place.member(GROUP - j), part, b).wait_recv()
        plane = plane_of(b, part)

        @pl.loop(0, quarter // 4)
        def _(k4):
            total = psrc[:, :basis]
            same = psrc[:, basis:basis + new]
            for i in range(4):
                y = k4 * 4 + i
                k = plane * quarter + y
                w = wt[plane, y]
                hi, lo = split(w)
                total = total + dot3(hi, lo, qh[k], ql[k], TRANSPOSED)
                same = same + lax.dot_general(
                    w, w, (TRANSPOSED, ((), ())), precision=HIGH, preferred_element_type=f32)
            psrc[:, :basis] = total
            psrc[:, basis:basis + new] = same

    preduce = Reducer(place, psrc, pfirst, psecond, pfull, [psem.at[i] for i in range(6)])
    preduce.start1()
    preduce.start2()
    preduce.start3()
    for part in (0, 1):
        for j in range(1, GROUP):
            to = place.member(j)
            copy_out(j, to, g, part, lax.rem(to, 2)).wait_send()
    preduce.finish()

    proj = pfull[:, :basis] * cell_weight
    own_gram = pfull[:, basis:basis + new] * cell_weight
    basis_gram = gfull[...] * cell_weight
    coef = proj + (proj - dot(proj, basis_gram))
    coef_ref[...] = coef
    coef_hi, coef_lo = split(coef)

    half = dot(coef, basis_gram) * 0.5 - proj
    turn = lax.dot_general(coef, half, (TRANSPOSED, ((), ())), precision=HIGH, preferred_element_type=f32)
    gram = own_gram + (turn + turn.T)

    r64 = lax.broadcasted_iota(jnp.int32, (new, new), 0)
    c64 = lax.broadcasted_iota(jnp.int32, (new, new), 1)
    eye = jnp.where(r64 == c64, 1.0, 0.0).astype(f32)
    work = jnp.concatenate([gram, eye], axis=1)
    per = new // cells
    for k in range(cells):
        for j in range(k * per, min((k + 1) * per, new - 1)):
            lo = (j // 8) * 8
            live = work[lo:]
            pivot_row = work[j:j + 1]
            scaled = pivot_row / pivot_row[:, j:j + 1]
            col = live[:, j:j + 1]
            below_pivot = lax.broadcasted_iota(jnp.int32, (new - lo, 1), 0) > (j - lo)
            live = live - jnp.where(below_pivot, col, 0.0) * scaled
            work = jnp.concatenate([work[:lo], live], axis=0) if lo else live
        w2 = wt[k // quarter, k % quarter] - dot3(coef_hi, coef_lo, qh[k], ql[k], PLAIN)
        wh[k], wl[k] = split(w2)
    diag = jnp.sum(jnp.where(r64 == c64, work[:, :new], 0.0), axis=1, keepdims=True)
    work = work / jnp.sqrt(diag)
    upper = jnp.where(c64 >= r64, work[:, :new], 0.0)
    fac_ref[...] = lax.dot_general(
        upper, eye, (((0,), (0,)), ((), ())), precision=HIGH, preferred_element_type=f32)
    inv_hi, inv_lo = split(work[:, new:])

    def result(k):
        return pltpu.make_async_copy(
            wt.at[k // quarter, k % quarter], out_ref.at[:, k // quarter, k % quarter, :], osem.at[k])

    for k in range(cells):
        wt[k // quarter, k % quarter] = dot3(inv_hi, inv_lo, wh[k], wl[k], PLAIN)
        result(k).start()
    for k in range(cells):
        result(k).wait()


def local(slabs, labels, conductance, capacity_table, shift_values, prior_basis):
    basis, slab_x, quarter, depth = prior_basis.shape
    shifts = shift_values.shape[0]
    new = shifts * COLS
    rows_y = labels.shape[1]
    cells = slab_x * quarter
    count = cells * depth * lax.axis_size("shift") * lax.axis_size("space")
    f32 = jnp.float32

    def reducer(rows, lanes):
        c = rows // GROUP
        return [pltpu.VMEM((rows, lanes), f32), pltpu.VMEM((GROUP - 1, c, lanes), f32),
                pltpu.VMEM((slabs, c, lanes), f32), pltpu.VMEM((rows, lanes), f32)]

    dma = pltpu.SemaphoreType.DMA
    width = max(GROUP, slabs)
    vmem = pl.BlockSpec(memory_space=pltpu.VMEM)
    block, coef, factor = pl.pallas_call(
        functools.partial(kernel, slabs, 1.0 / count),
        out_shape=[
            jax.ShapeDtypeStruct((new, slab_x, quarter, depth), f32),
            jax.ShapeDtypeStruct((new, basis), f32),
            jax.ShapeDtypeStruct((new, new), f32),
        ],
        in_specs=[pl.BlockSpec(memory_space=pltpu.HBM)] * 5,
        out_specs=[vmem] * 3,
        scratch_shapes=[
            pltpu.VMEM((6, rows_y, depth), jnp.int32),
            pltpu.VMEM((6, rows_y, depth), f32),
            pltpu.VMEM((4, rows_y, depth), f32),
            pltpu.VMEM((6, 4, rows_y, depth), f32),
            pltpu.VMEM((4, rows_y, depth), f32),
            pltpu.VMEM((4, rows_y, depth), f32),
            pltpu.VMEM((4, rows_y, COLS, depth), f32),
            pltpu.VMEM((4, rows_y, COLS, depth), f32),
            pltpu.VMEM((SWEEPS - 1, 6, rows_y + 2, COLS, depth), f32),
            pltpu.VMEM((slab_x, quarter, new, depth), f32),
            pltpu.VMEM((basis, slab_x, quarter, depth), f32),
            pltpu.VMEM((slab_x, quarter, basis, depth), f32),
            pltpu.VMEM((cells, basis, depth), jnp.bfloat16),
            pltpu.VMEM((cells, basis, depth), jnp.bfloat16),
            pltpu.VMEM((cells, new, depth), jnp.bfloat16),
            pltpu.VMEM((cells, new, depth), jnp.bfloat16),
            *reducer(basis, basis),
            *reducer(new, basis + 128),
            pltpu.VMEM((basis, basis), f32),
            pltpu.SMEM(conductance.shape, f32),
            pltpu.SMEM(capacity_table.shape, f32),
            pltpu.SMEM(shift_values.shape, f32),
            dma((3,)), dma((3,)), dma((2, GROUP - 1)), dma((2, GROUP - 1)),
            dma((2, GROUP - 1)), dma((2, GROUP - 1)), dma((SWEEPS - 1, 2)), dma((SWEEPS - 1, 2)),
            dma((10,)), dma((2, cells)), dma((cells,)),
            dma((6, width)), dma((6, width)),
        ],
        compiler_params=pltpu.CompilerParams(
            collective_id=0, has_side_effects=True, vmem_limit_bytes=64 * 1024 * 1024),
    )(labels, conductance, capacity_table, shift_values, prior_basis)
    return block.reshape(shifts, COLS, slab_x, quarter, depth), coef, factor


def solution(mesh):
    in_specs = (P("space", None, None), P(), P(), P(), P(None, "space", "shift", None))
    out_specs = (P(None, None, "space", "shift", None), P(), P())
    slabs = mesh.shape["space"] // 2
    return jax.shard_map(
        functools.partial(local, slabs), mesh=mesh, in_specs=in_specs, out_specs=out_specs, check_vma=False)
```

```python
import functools

import jax
import jax.numpy as jnp
from jax import lax
from jax.experimental import pallas as pl
from jax.experimental.pallas import tpu as pltpu
from jax.sharding import PartitionSpec as P

COLS = 8
SWEEPS = 4
GROUP = 8
LOWER_BOUND = 0.1
UPPER_BOUND = 2.0
MESH = pl.DeviceIdType.MESH
HIGH = lax.Precision.HIGHEST


def dot(a, b):
    return lax.dot_general(
        a, b, (((1,), (0,)), ((), ())), precision=HIGH, preferred_element_type=jnp.float32
    )


class Reducer:
    def __init__(self, place, src, first, second, full, sems):
        self.place, self.src, self.first, self.second, self.full = place, src, first, second, full
        self.s1, self.r1, self.s2, self.r2, self.s3, self.r3 = sems
        self.chunk = src.shape[0] // GROUP

    def rows(self, t):
        return pl.ds(pl.multiple_of(t * self.chunk, 8), self.chunk)

    def copy1(self, j):
        t = self.place.member(j)
        return pltpu.make_async_remote_copy(
            self.src.at[self.rows(t)], self.first.at[j - 1], self.s1.at[j - 1], self.r1.at[j - 1],
            device_id=self.place.group_id(t), device_id_type=MESH)

    def copy2(self, j, slot, to):
        return pltpu.make_async_remote_copy(
            self.second.at[slot], self.second.at[slot], self.s2.at[j - 1], self.r2.at[slot],
            device_id=self.place.slab_id(to), device_id_type=MESH)

    def copy3(self, j, owner):
        t = self.place.member(j)
        return pltpu.make_async_remote_copy(
            self.full.at[self.rows(owner)], self.full.at[self.rows(owner)],
            self.s3.at[j - 1], self.r3.at[j - 1],
            device_id=self.place.group_id(t), device_id_type=MESH)

    def start1(self):
        for j in range(1, GROUP):
            self.copy1(j).start()

    def start2(self):
        place = self.place
        total = self.src[self.rows(place.g)]
        for j in range(1, GROUP):
            self.copy1(j).wait_recv()
            total = total + self.first[j - 1]
        self.second[place.z] = total
        for j in range(1, place.slabs):
            self.copy2(j, place.z, lax.rem(place.z + j, place.slabs)).start()

    def start3(self):
        place = self.place
        for j in range(1, place.slabs):
            other = lax.rem(place.z + j, place.slabs)
            self.copy2(j, other, other).wait_recv()
        total = self.second[0]
        for i in range(1, place.slabs):
            total = total + self.second[i]
        self.full[self.rows(place.g)] = total
        for j in range(1, GROUP):
            self.copy3(j, place.g).start()

    def finish(self):
        place = self.place
        for j in range(1, GROUP):
            self.copy3(j, place.member(GROUP - j)).wait_recv()
        for j in range(1, GROUP):
            self.copy1(j).wait_send()
            self.copy3(j, place.g).wait_send()
        for j in range(1, place.slabs):
            self.copy2(j, place.z, lax.rem(place.z + j, place.slabs)).wait_send()


class Place:
    def __init__(self, slabs):
        self.s = lax.axis_index("shift")
        self.p = lax.axis_index("space")
        self.b = lax.rem(self.p, 2)
        self.z = self.p // 2
        self.g = self.s * 2 + self.b
        self.slabs = slabs

    def member(self, j):
        return lax.rem(self.g + j, GROUP)

    def group_id(self, t):
        return (t // 2, self.z * 2 + lax.rem(t, 2))

    def slab_id(self, z):
        return (self.s, z * 2 + self.b)


def split(x):
    hi = x.astype(jnp.bfloat16)
    return hi, (x - hi.astype(jnp.float32)).astype(jnp.bfloat16)


def raw(a, b, dims):
    return lax.dot_general(a, b, (dims, ((), ())), preferred_element_type=jnp.float32)


def dot3(a_hi, a_lo, b_hi, b_lo, dims):
    rows = a_hi.shape[0]
    both = raw(jnp.concatenate([a_hi, a_lo], axis=0), b_hi, dims)
    return both[:rows] + (both[rows:] + raw(a_hi, b_lo, dims))


TRANSPOSED = ((1,), (1,))
PLAIN = ((1,), (0,))


def kernel(slabs, cell_weight, labels_hbm, cond_hbm, capa_hbm, shift_hbm, q_hbm,
           out_ref, coef_ref, fac_ref,
           lab, kap, cap, face, dg, rc, rem, sol, dirs, wt, qn, qs, qh, ql, wh, wl,
           gsrc, gfirst, gsecond, gfull, psrc, pfirst, psecond, pfull,
           cross, cond_ref, capa_ref, shift_ref,
           lab_s, lab_r, in_s, in_r, out_s, out_r, halo_s, halo_r, loc, qsem, osem, gsem, psem):
    place = Place(slabs)
    s, b, z, g = place.s, place.b, place.z, place.g
    f32 = jnp.float32
    basis, slab_x, quarter, depth = q_hbm.shape
    new = wt.shape[2]
    cells = slab_x * quarter
    rows_y = lab.shape[1]
    old = basis - new

    def load(k, first, count, i):
        return pltpu.make_async_copy(
            qn.at[pl.ds(first, count), k // quarter, k % quarter, :],
            qs.at[k // quarter, k % quarter, pl.ds(first, count), :], qsem.at[i, k])

    fetch = [pltpu.make_async_copy(q_hbm.at[pl.ds(first, count)], qn.at[pl.ds(first, count)], loc.at[6 + i])
             for i, (first, count) in enumerate([(old, new), (0, old)])]
    fetch[0].start()
    own_lab = pltpu.make_async_copy(labels_hbm, lab.at[pl.ds(1 + 2 * b, 2)], loc.at[2])
    own_lab.start()
    tables = [pltpu.make_async_copy(src, dst, loc.at[3 + i]) for i, (src, dst) in enumerate(
        [(cond_hbm, cond_ref), (capa_hbm, capa_ref), (shift_hbm, shift_ref)])]
    for copy in tables:
        copy.start()
    fetch[1].start()
    fetch[0].wait()
    for k in range(cells):
        load(k, old, new, 0).start()

    barrier = pltpu.get_barrier_semaphore()
    for j in range(1, GROUP):
        pl.semaphore_signal(barrier, inc=1, device_id=place.group_id(place.member(j)), device_id_type=MESH)
    for j in range(1, slabs):
        pl.semaphore_signal(barrier, inc=1, device_id=place.slab_id(lax.rem(z + j, slabs)), device_id_type=MESH)
    for n in range(SWEEPS - 1):
        for i in range(1, 5):
            dirs[n, i, 0] = jnp.zeros((COLS, depth), f32)
            dirs[n, i, rows_y + 1] = jnp.zeros((COLS, depth), f32)
    pl.semaphore_wait(barrier, GROUP - 1 + slabs - 1)

    pair = lax.rem(b + 1, 2)

    def lab_pair(owner):
        return pltpu.make_async_remote_copy(
            labels_hbm, lab.at[pl.ds(1 + 2 * owner, 2)], lab_s.at[0], lab_r.at[0],
            device_id=(s, z * 2 + pair), device_id_type=MESH)

    def edge(from_plane, to_plane, k, to):
        return pltpu.make_async_remote_copy(
            lab.at[from_plane], lab.at[to_plane], lab_s.at[k], lab_r.at[k],
            device_id=place.slab_id(to), device_id_type=MESH)

    def plane_of(member_b, part):
        return member_b if part == 0 else 1 - member_b

    def column(t):
        return pl.ds(pl.multiple_of(t * COLS, COLS), COLS)

    def slot(field, t, part):
        tb = lax.rem(t, 2)
        return field.at[2 * tb + plane_of(tb, part), pl.ds((t // 2) * quarter, quarter)]

    def tail(t, part):
        return qs.at[plane_of(b, part), :, pl.ds(pl.multiple_of(old + t * COLS, COLS), COLS), :]

    def copy_in(j, to, owner, part):
        return pltpu.make_async_remote_copy(
            tail(to, part), slot(rem, owner, part), in_s.at[part, j - 1], in_r.at[part, j - 1],
            device_id=place.group_id(to), device_id_type=MESH)

    lab_pair(b).start()
    for k in range(cells):
        load(k, old, new, 0).wait()
    for part in (0, 1):
        for j in range(1, GROUP):
            copy_in(j, place.member(j), g, part).start()
    mine = [pltpu.make_async_copy(tail(g, part), slot(rem, g, part), loc.at[8 * part]) for part in (0, 1)]
    for copy in mine:
        copy.start()
    fetch[1].wait()
    for k in range(cells):
        load(k, 0, old, 1).start()
    own_lab.wait()
    lab_pair(pair).wait_recv()

    @pl.when(z > 0)
    def _():
        edge(1, 5, 1, z - 1).start()

    @pl.when(z < slabs - 1)
    def _():
        edge(4, 0, 2, z + 1).start()

    for end, there in ((0, z == 0), (5, z == slabs - 1)):
        @pl.when(there)
        def _():
            lab[end] = jnp.full((rows_y, depth), -1, jnp.int32)
            for n in range(SWEEPS - 1):
                dirs[n, end] = jnp.zeros((rows_y + 2, COLS, depth), f32)

    for k in range(cells):
        load(k, 0, old, 1).wait()
    gsrc[...] = jnp.zeros_like(gsrc)
    cross[...] = jnp.zeros_like(cross)

    @pl.loop(0, cells)
    def _(k):
        hi, lo = split(qs[k // quarter, lax.rem(k, quarter)])
        qh[k] = hi
        ql[k] = lo
        gsrc[...] += raw(hi, hi, TRANSPOSED)
        cross[...] += raw(hi, lo, TRANSPOSED)

    gsrc[...] += cross[...] + cross[...].T

    @pl.when(z > 0)
    def _():
        edge(4, 0, 2, z - 1).wait_recv()

    @pl.when(z < slabs - 1)
    def _():
        edge(1, 5, 1, z + 1).wait_recv()

    for copy in tables:
        copy.wait()

    @pl.loop(0, 6)
    def _(i):
        value = lab[i]
        k_acc = jnp.zeros((rows_y, depth), f32)
        for m in range(cond_ref.shape[0]):
            k_acc = jnp.where(value == m, cond_ref[m], k_acc)
        kap[i] = k_acc

    shift = shift_ref[g]
    row = lax.broadcasted_iota(jnp.int32, (rows_y, depth), 0)
    lane = lax.broadcasted_iota(jnp.int32, (rows_y, depth), 1)

    @pl.loop(0, 4)
    def _(i):
        value = lab[i + 1]
        c_acc = jnp.zeros((rows_y, depth), f32)
        for m in range(capa_ref.shape[0]):
            c_acc = jnp.where(value == m, capa_ref[m], c_acc)
        cap[i] = c_acc
        me = kap[i + 1]
        zero = jnp.zeros_like(me)
        west = 0.5 * (me + kap[i])
        east = 0.5 * (me + kap[i + 2])
        south = 0.5 * (me + jnp.where(row == 0, zero, pltpu.roll(me, 1, 0)))
        north = 0.5 * (me + jnp.where(row == rows_y - 1, zero, pltpu.roll(me, rows_y - 1, 0)))
        below = 0.5 * (me + jnp.where(lane == 0, zero, pltpu.roll(me, 1, 1)))
        above = 0.5 * (me + jnp.where(lane == depth - 1, zero, pltpu.roll(me, depth - 1, 1)))
        diag = ((west + east) + (south + north)) + (below + above) + shift * c_acc
        dg[i] = diag
        rc[i] = 1.0 / diag
        face[0, i] = west
        face[1, i] = east
        face[2, i] = south
        face[3, i] = north
        face[4, i] = jnp.where(lane == 0, zero, below)
        face[5, i] = jnp.where(lane == depth - 1, zero, above)

    greduce = Reducer(place, gsrc, gfirst, gsecond, gfull, [gsem.at[i] for i in range(6)])

    def arrived(part):
        mine[part].wait()
        for j in range(1, GROUP):
            copy_in(j, place.member(j), place.member(GROUP - j), part).wait_recv()

    center = 0.5 * (UPPER_BOUND + LOWER_BOUND)
    spread = 0.5 * (UPPER_BOUND - LOWER_BOUND)
    ratio = center / spread

    def begin(i):
        @pl.loop(0, rows_y // 8)
        def _(t):
            tile = pl.ds(pl.multiple_of(t * 8, 8), 8)
            c_t, rc_t = cap[i, tile], rc[i, tile]
            for u in range(8):
                y = t * 8 + u
                r = rem[i, y] * c_t[u:u + 1]
                d = (rc_t[u:u + 1] * r) / center
                rem[i, y] = r
                sol[i, y] = d
                dirs[0, i + 1, y + 1] = d

    def sweep(n, i, keep, step):
        @pl.loop(0, rows_y // 8)
        def _(t):
            tile = pl.ds(pl.multiple_of(t * 8, 8), 8)
            f = [face[k, i, tile] for k in range(6)]
            dg_t, rc_t = dg[i, tile], rc[i, tile]
            for u in range(8):
                y = t * 8 + u
                w_, e_, s_, n_, b_, a_ = [v[u:u + 1] for v in f]
                d = dirs[n, i + 1, y + 1]
                near = w_ * dirs[n, i, y + 1] + e_ * dirs[n, i + 2, y + 1]
                near = near + s_ * dirs[n, i + 1, y] + n_ * dirs[n, i + 1, y + 2]
                near = near + b_ * pltpu.roll(d, 1, 1) + a_ * pltpu.roll(d, depth - 1, 1)
                r = rem[i, y] - (dg_t[u:u + 1] * d - near)
                nd = keep * d + step * (rc_t[u:u + 1] * r)
                sol[i, y] = sol[i, y] + nd
                if n + 1 < SWEEPS - 1:
                    rem[i, y] = r
                    dirs[n + 1, i + 1, y + 1] = nd

    def halo(n, src, dst, k, to):
        return pltpu.make_async_remote_copy(
            dirs.at[n, src, pl.ds(1, rows_y)], dirs.at[n, dst, pl.ds(1, rows_y)],
            halo_s.at[n, k], halo_r.at[n, k], device_id=place.slab_id(to), device_id_type=MESH)

    def send_halo(n):
        @pl.when(z > 0)
        def _():
            halo(n, 1, 5, 0, z - 1).start()

        @pl.when(z < slabs - 1)
        def _():
            halo(n, 4, 0, 1, z + 1).start()

    arrived(0)
    begin(0)
    begin(3)
    send_halo(0)
    arrived(1)
    greduce.start1()
    begin(1)
    begin(2)
    def copy_out(j, to, owner, part, reader_b):
        return pltpu.make_async_remote_copy(
            slot(sol, to, part), wt.at[plane_of(reader_b, part), :, column(owner), :],
            out_s.at[part, j - 1], out_r.at[part, j - 1],
            device_id=place.group_id(to), device_id_type=MESH)

    back = [pltpu.make_async_copy(
        slot(sol, g, part), wt.at[plane_of(b, part), :, column(g), :], loc.at[1 + 8 * part]) for part in (0, 1)]

    def send_out(part):
        for j in range(1, GROUP):
            to = place.member(j)
            copy_out(j, to, g, part, lax.rem(to, 2)).start()
        back[part].start()

    weight_old = 1.0 / ratio
    for n in range(SWEEPS - 1):
        weight = 1.0 / (2.0 * ratio - weight_old)
        keep, step = weight * weight_old, 2.0 * weight / spread
        weight_old = weight
        sweep(n, 1, keep, step)
        sweep(n, 2, keep, step)
        if n == SWEEPS - 2:
            send_out(1)

        @pl.when(z > 0)
        def _():
            halo(n, 4, 0, 1, z - 1).wait_recv()

        @pl.when(z < slabs - 1)
        def _():
            halo(n, 1, 5, 0, z + 1).wait_recv()

        sweep(n, 0, keep, step)
        sweep(n, 3, keep, step)
        if n + 1 < SWEEPS - 1:
            send_halo(n + 1)

    send_out(0)
    greduce.start2()

    lab_pair(b).wait_send()

    @pl.when(z > 0)
    def _():
        edge(1, 5, 1, z - 1).wait_send()
        for n in range(SWEEPS - 1):
            halo(n, 1, 5, 0, z - 1).wait_send()

    @pl.when(z < slabs - 1)
    def _():
        edge(4, 0, 2, z + 1).wait_send()
        for n in range(SWEEPS - 1):
            halo(n, 4, 0, 1, z + 1).wait_send()

    for part in (0, 1):
        for j in range(1, GROUP):
            copy_in(j, place.member(j), g, part).wait_send()
    psrc[...] = jnp.zeros_like(psrc)
    for part in (1, 0):
        back[part].wait()
        for j in range(1, GROUP):
            copy_out(j, place.member(j), place.member(GROUP - j), part, b).wait_recv()
        plane = plane_of(b, part)

        @pl.loop(0, quarter // 4)
        def _(k4):
            total = psrc[:, :basis]
            same = psrc[:, basis:basis + new]
            for i in range(4):
                y = k4 * 4 + i
                k = plane * quarter + y
                w = wt[plane, y]
                hi, lo = split(w)
                total = total + dot3(hi, lo, qh[k], ql[k], TRANSPOSED)
                same = same + lax.dot_general(
                    w, w, (TRANSPOSED, ((), ())), precision=HIGH, preferred_element_type=f32)
            psrc[:, :basis] = total
            psrc[:, basis:basis + new] = same

    preduce = Reducer(place, psrc, pfirst, psecond, pfull, [psem.at[i] for i in range(6)])
    preduce.start1()
    greduce.start3()
    preduce.start2()
    preduce.start3()
    greduce.finish()
    for part in (0, 1):
        for j in range(1, GROUP):
            to = place.member(j)
            copy_out(j, to, g, part, lax.rem(to, 2)).wait_send()
    preduce.finish()

    proj = pfull[:, :basis] * cell_weight
    own_gram = pfull[:, basis:basis + new] * cell_weight
    basis_gram = gfull[...] * cell_weight
    coef = proj + (proj - dot(proj, basis_gram))
    coef_ref[...] = coef
    coef_hi, coef_lo = split(coef)

    half = dot(coef, basis_gram) * 0.5 - proj
    turn = lax.dot_general(coef, half, (TRANSPOSED, ((), ())), precision=HIGH, preferred_element_type=f32)
    gram = own_gram + (turn + turn.T)

    r64 = lax.broadcasted_iota(jnp.int32, (new, new), 0)
    c64 = lax.broadcasted_iota(jnp.int32, (new, new), 1)
    eye = jnp.where(r64 == c64, 1.0, 0.0).astype(f32)
    work = jnp.concatenate([gram, eye], axis=1)
    per = new // cells
    for k in range(cells):
        for j in range(k * per, min((k + 1) * per, new - 1)):
            lo = (j // 8) * 8
            live = work[lo:]
            pivot_row = work[j:j + 1]
            scaled = pivot_row / pivot_row[:, j:j + 1]
            col = live[:, j:j + 1]
            below_pivot = lax.broadcasted_iota(jnp.int32, (new - lo, 1), 0) > (j - lo)
            live = live - jnp.where(below_pivot, col, 0.0) * scaled
            work = jnp.concatenate([work[:lo], live], axis=0) if lo else live
        w2 = wt[k // quarter, k % quarter] - dot3(coef_hi, coef_lo, qh[k], ql[k], PLAIN)
        wh[k], wl[k] = split(w2)
    diag = jnp.sum(jnp.where(r64 == c64, work[:, :new], 0.0), axis=1, keepdims=True)
    work = work / jnp.sqrt(diag)
    upper = jnp.where(c64 >= r64, work[:, :new], 0.0)
    fac_ref[...] = lax.dot_general(
        upper, eye, (((0,), (0,)), ((), ())), precision=HIGH, preferred_element_type=f32)
    inv_hi, inv_lo = split(work[:, new:])

    def result(k):
        return pltpu.make_async_copy(
            wt.at[k // quarter, k % quarter], out_ref.at[:, k // quarter, k % quarter, :], osem.at[k])

    for k in range(cells):
        wt[k // quarter, k % quarter] = dot3(inv_hi, inv_lo, wh[k], wl[k], PLAIN)
        result(k).start()
    for k in range(cells):
        result(k).wait()


def local(slabs, labels, conductance, capacity_table, shift_values, prior_basis):
    basis, slab_x, quarter, depth = prior_basis.shape
    shifts = shift_values.shape[0]
    new = shifts * COLS
    rows_y = labels.shape[1]
    cells = slab_x * quarter
    count = cells * depth * lax.axis_size("shift") * lax.axis_size("space")
    f32 = jnp.float32

    def reducer(rows, lanes):
        c = rows // GROUP
        return [pltpu.VMEM((rows, lanes), f32), pltpu.VMEM((GROUP - 1, c, lanes), f32),
                pltpu.VMEM((slabs, c, lanes), f32), pltpu.VMEM((rows, lanes), f32)]

    dma = pltpu.SemaphoreType.DMA
    width = max(GROUP, slabs)
    vmem = pl.BlockSpec(memory_space=pltpu.VMEM)
    block, coef, factor = pl.pallas_call(
        functools.partial(kernel, slabs, 1.0 / count),
        out_shape=[
            jax.ShapeDtypeStruct((new, slab_x, quarter, depth), f32),
            jax.ShapeDtypeStruct((new, basis), f32),
            jax.ShapeDtypeStruct((new, new), f32),
        ],
        in_specs=[pl.BlockSpec(memory_space=pltpu.HBM)] * 5,
        out_specs=[vmem] * 3,
        scratch_shapes=[
            pltpu.VMEM((6, rows_y, depth), jnp.int32),
            pltpu.VMEM((6, rows_y, depth), f32),
            pltpu.VMEM((4, rows_y, depth), f32),
            pltpu.VMEM((6, 4, rows_y, depth), f32),
            pltpu.VMEM((4, rows_y, depth), f32),
            pltpu.VMEM((4, rows_y, depth), f32),
            pltpu.VMEM((4, rows_y, COLS, depth), f32),
            pltpu.VMEM((4, rows_y, COLS, depth), f32),
            pltpu.VMEM((SWEEPS - 1, 6, rows_y + 2, COLS, depth), f32),
            pltpu.VMEM((slab_x, quarter, new, depth), f32),
            pltpu.VMEM((basis, slab_x, quarter, depth), f32),
            pltpu.VMEM((slab_x, quarter, basis, depth), f32),
            pltpu.VMEM((cells, basis, depth), jnp.bfloat16),
            pltpu.VMEM((cells, basis, depth), jnp.bfloat16),
            pltpu.VMEM((cells, new, depth), jnp.bfloat16),
            pltpu.VMEM((cells, new, depth), jnp.bfloat16),
            *reducer(basis, basis),
            *reducer(new, basis + 128),
            pltpu.VMEM((basis, basis), f32),
            pltpu.SMEM(conductance.shape, f32),
            pltpu.SMEM(capacity_table.shape, f32),
            pltpu.SMEM(shift_values.shape, f32),
            dma((3,)), dma((3,)), dma((2, GROUP - 1)), dma((2, GROUP - 1)),
            dma((2, GROUP - 1)), dma((2, GROUP - 1)), dma((SWEEPS - 1, 2)), dma((SWEEPS - 1, 2)),
            dma((10,)), dma((2, cells)), dma((cells,)),
            dma((6, width)), dma((6, width)),
        ],
        compiler_params=pltpu.CompilerParams(
            collective_id=0, has_side_effects=True, vmem_limit_bytes=64 * 1024 * 1024),
    )(labels, conductance, capacity_table, shift_values, prior_basis)
    return block.reshape(shifts, COLS, slab_x, quarter, depth), coef, factor


def solution(mesh):
    in_specs = (P("space", None, None), P(), P(), P(), P(None, "space", "shift", None))
    out_specs = (P(None, None, "space", "shift", None), P(), P())
    slabs = mesh.shape["space"] // 2
    return jax.shard_map(
        functools.partial(local, slabs), mesh=mesh, in_specs=in_specs, out_specs=out_specs, check_vma=False)
```
